256 devices in a mesh: ctx: 32 (over x, z), exp: 8 (over y, core).
Axes of the slice: x: 4, y: 4, z: 8, core: 2. Of those that a mesh axis runs over, the one named last changes fastest.
Arguments:
- queries: bfloat16 [2048, 2, 8192], P('ctx', None, 'exp'), may hold values from -6 to 6
- key_vecs: bfloat16 [2048, 2, 8192], P('ctx', None, 'exp'), may hold values from -6 to 6
- values: bfloat16 [2048, 2, 8192], P('ctx', None, 'exp'), may hold values from -6 to 6
- seq_lengths: int32 [2], replicated, may hold values from 1 to 2048, 3072 in all
- head_gain: bfloat16 [8192], P('exp'), may hold values from 0.099609375 to 1.8984375
- out_weight: bfloat16 [8192, 3072], P('exp'), may hold values from -0.0625 to 0.0625
- residual: bfloat16 [2048, 2, 3072], P(('ctx', 'exp')), may hold values from -6 to 6
- norm_gain: bfloat16 [3072], replicated, may hold values from 0.099609375 to 1.8984375
- expert_ids: int32 [2048, 2, 2], P(('ctx', 'exp')), may hold values from 0 to 7, all different within a row; in each aligned block of 16 rows (0 to 15, 16 to 31, ..., all dimensions but the last counted through in order) at most 6 rows name the same one
- gate_weights: float32 [2048, 2, 2], P(('ctx', 'exp')), may hold values from 0.25 to 1
- gate_weight: bfloat16 [8, 3072, 9216], P('exp', None, 'ctx'), may hold values from -0.109375 to 0.109375
- up_weight: bfloat16 [8, 3072, 9216], P('exp', None, 'ctx'), may hold values from -0.109375 to 0.109375
- down_weight: bfloat16 [8, 9216, 3072], P('exp', 'ctx'), may hold values from -0.125 to 0.125
Outputs:
- layer_out: bfloat16 [2048, 2, 3072], P(('ctx', 'exp'))
The draws below stay inside these ranges and needn't reach their ends.
Inputs may be any that keep to these rules, and one draw needn't show every extreme that they name: `expert_ids`: tokens are taken in order of position, then sequence; in each aligned block of 16 tokens (the rows of one device) no expert is named by more than 6 routes, a bound that some block reaches; the two experts of a token differ.
All inputs are finite; a program needn't handle non-finite values.
Results may differ from the reference program's by a relative error of at most 0.03.
Values may be sent and summed in bfloat16 or wider, within the bound.
No kernel may reach another device: no remote copies, remote signals or barrier semaphores. Data moves between devices by JAX's collectives and lax.ppermute only.
A program may use at most 128 MiB of HBM per device.

```python
import math
import jax
import jax.numpy as jnp
import numpy as np
from jax import lax

D = 3072
HEADS = 64
HDIM = 128
FF = 9216
SEQS = 2
CH = 64
EXPERTS = 8
LEN = 2048
TOKENS = 4096
TOK_DEV = 16
MOST = 6
N_CTX = 32


def block_scale(own_key, extent, cuts, least, top_value):
    loudness = 1.0
    for axis_at, parts in cuts:
        draws = jax.random.uniform(jax.random.fold_in(jax.random.fold_in(own_key, 6), axis_at), (parts,), jnp.float32, least / len(cuts), top_value / len(cuts))
        loudness = loudness * jnp.repeat(jnp.exp(draws), extent[axis_at] // parts).reshape((-1,) + (1,) * (len(extent) - 1 - axis_at))
    return loudness


def profile(number_of, total, bound, slope):
    portions = [(1 << 20) // math.isqrt(grade ** slope) + 1 for grade in range(2, number_of + 1)]
    surplus, given = total - bound - (number_of - 1), [1] * (number_of - 1)
    while surplus > 0:
        movable = [i for i in range(number_of - 1) if given[i] < bound]
        pool, left = sum([portions[i] for i in movable]), surplus
        for i in movable:
            more = min(bound - given[i], max(1, left * portions[i] // pool), surplus)
            given[i] = given[i] + more
            surplus = surplus - more
    return np.array([bound] + given)


def ragged_sizes(stream_key, number_of, total, most, slope):
    if number_of == 2:
        one = jax.random.randint(stream_key, (), max(1, total - most), min(most, total - 1) + 1)
        return jnp.stack([one, total - one])
    sizes = jnp.asarray(profile(number_of, total, most, slope), jnp.int32)
    couples = (number_of - 1) // 2
    giver, receiver = sizes[1:1 + 2 * couples:2], sizes[2:2 + 2 * couples:2]
    room = jnp.minimum(giver - 1, most - receiver)
    passed = jax.random.randint(jax.random.fold_in(stream_key, 1), (couples,), 0, 1 << 20) % (room + 1)
    sizes = sizes.at[1:1 + 2 * couples:2].set(giver - passed).at[2:2 + 2 * couples:2].set(receiver + passed)
    return sizes[jax.random.permutation(jax.random.fold_in(stream_key, 2), number_of)]


def deal_out(key, own, number, rows, amount, top, reach, slope):
    sequence = jax.random.permutation(key, amount)
    crowded, ordinary = portions_of(amount, rows * top, reach, slope, True), portions_of(amount, rows * top, reach, slope, False)
    places = jnp.arange(amount)

    def named(lengths, turn):
        used = int((lengths > 0).sum())
        fixed = max(1, used // 4)
        passed = fixed + (places - fixed + turn * (used - fixed)) % max(1, amount - fixed)
        return jnp.zeros((amount,), jnp.int32).at[sequence[jnp.where(places < fixed, places, passed)]].set(jnp.asarray(lengths, jnp.int32))

    lengths = jnp.where(number % 4 == 0, named(crowded, number // 4), named(ordinary, number - number // 4 - 1))
    mixed = jax.random.permutation(jax.random.fold_in(own, 3), amount)
    source_of, receiver = mixed[0:amount // 2 * 2:2], mixed[1:amount // 2 * 2:2]
    room = jnp.minimum(lengths[source_of] - 1, reach - lengths[receiver]) // 2
    room = jnp.where((source_of == sequence[0]) | (receiver == sequence[0]) | (lengths[receiver] == 0), 0, jnp.maximum(room, 0))
    passed = jax.random.randint(jax.random.fold_in(own, 4), (amount // 2,), 0, 1 << 20) % (room + 1)
    lengths = lengths.at[source_of].add(-passed).at[receiver].add(passed)
    labels = jnp.searchsorted(jnp.cumsum(lengths), jnp.arange(rows * top), side="right").astype(jnp.int32)
    grid = labels.reshape(top, rows).T
    grid = grid[jax.random.permutation(jax.random.fold_in(own, 1), rows)]
    turn = jax.random.randint(jax.random.fold_in(own, 2), (rows, 1), 0, top)
    return jnp.take_along_axis(grid, (jnp.arange(top)[None, :] + turn) % top, axis=1)


def portions_of(number_of, total, bound, slope, full):
    portions = [(1 << 20) // math.isqrt(grade ** slope) + 1 for grade in range(1, number_of + 1)]
    largest = bound if full else min(bound, max(-(-total // number_of), total * portions[0] // sum(portions)))
    least = 1 if total - largest >= number_of - 1 else 0
    given, rest = [largest] + [least] * (number_of - 1), total - largest - least * (number_of - 1)
    while rest > 0:
        movable = [i for i in range(1, number_of) if given[i] < largest] or [i for i in range(1, number_of) if given[i] < bound]
        mass, left = sum([portions[i] for i in movable]), rest
        for i in movable:
            addition = min(bound - given[i], max(1, left * portions[i] // mass), rest)
            given[i] = given[i] + addition
            rest = rest - addition
    return np.array(given)


def noise(stream_key, dims, width, limit, pieces=(), kind=jnp.bfloat16):
    array = jax.random.normal(stream_key, dims, jnp.float32) * width
    if len(pieces) > 0:
        array = block_scale(stream_key, dims, pieces, -0.22, 0.18) * array
    return jnp.clip(array, min=-limit, max=limit).astype(kind)


def setup_inputs(seed: int = 0) -> dict:
    key_of = jax.random.split(jax.random.key(seed), 14)
    queries = noise(key_of[0], (LEN, SEQS, HEADS * HDIM), 1.0, 6.0, ((0, 32), (2, 8)))
    key_vecs = noise(key_of[1], (LEN, SEQS, HEADS * HDIM), 1.0, 6.0, ((0, 32), (2, 8)))
    values = noise(key_of[2], (LEN, SEQS, HEADS * HDIM), 1.0, 6.0, ((0, 32), (2, 8)))
    seq_lengths = ragged_sizes(key_of[3], SEQS, 3 * LEN // 2, LEN, 0).astype(jnp.int32)
    head_gain = jnp.clip(1.0 + 0.18 * jax.random.normal(key_of[4], (HEADS * HDIM,), jnp.float32), 0.099609375, 1.8984375).astype(jnp.bfloat16)
    out_weight = noise(key_of[5], (HEADS * HDIM, D), (HEADS * HDIM) ** -0.5, 0.0625, ((0, 8),))
    residual = noise(key_of[6], (LEN, SEQS, D), 1.0, 6.0, ((0, 256),))
    norm_gain = jnp.clip(1.0 + 0.18 * jax.random.normal(key_of[7], (D,), jnp.float32), 0.099609375, 1.8984375).astype(jnp.bfloat16)
    expert_ids_keys = jax.random.split(jax.random.fold_in(key_of[8], 1), LEN * SEQS // TOK_DEV)
    expert_ids_turns = jax.random.permutation(jax.random.fold_in(key_of[8], 3), LEN * SEQS // TOK_DEV)
    expert_ids = jax.vmap(lambda own, number: deal_out(jax.random.fold_in(key_of[8], 2), own, number, TOK_DEV, EXPERTS, 2, MOST, 2))(expert_ids_keys, expert_ids_turns).reshape((LEN, SEQS, 2))
    gate_weights = jnp.clip(0.25 + 0.75 * jax.random.uniform(key_of[9], (LEN, SEQS, 2), jnp.float32) ** block_scale(key_of[9], (LEN, SEQS, 2), ((0, 256),), -0.2, 0.2), 0.25, 1.0)
    gate_weight = noise(key_of[10], (EXPERTS, D, FF), D ** -0.5, 0.109375, ((0, 8), (2, 32)))
    up_weight = noise(key_of[11], (EXPERTS, D, FF), D ** -0.5, 0.109375, ((0, 8), (2, 32)))
    down_weight = noise(key_of[12], (EXPERTS, FF, D), (FF // 4) ** -0.5, 0.125, ((0, 8), (1, 32)))
    return {"queries": queries, "key_vecs": key_vecs, "values": values, "seq_lengths": seq_lengths, "head_gain": head_gain, "out_weight": out_weight, "residual": residual, "norm_gain": norm_gain, "expert_ids": expert_ids, "gate_weights": gate_weights, "gate_weight": gate_weight, "up_weight": up_weight, "down_weight": down_weight}


epsilon = 1e-05
highest = lax.Precision.HIGHEST

def rounded(array_in):
    return lax.optimization_barrier(array_in.astype(jnp.bfloat16)).astype(jnp.float32)

def reference(queries, key_vecs, values, seq_lengths, head_gain, out_weight, residual, norm_gain, expert_ids, gate_weights, gate_weight, up_weight, down_weight):
    query_blocks = queries.reshape(N_CTX, CH, SEQS, HEADS, HDIM)
    key_blocks = key_vecs.reshape(N_CTX, CH, SEQS, HEADS, HDIM)
    value_blocks = values.reshape(N_CTX, CH, SEQS, HEADS, HDIM)
    position = jnp.arange(LEN, dtype=jnp.int32).reshape(N_CTX, CH)
    live_keys = position[:, :, None] < seq_lengths[None, None, :]
    key_blocks = jnp.where(live_keys[:, :, :, None, None], key_blocks, jnp.zeros_like(key_blocks))
    head_gains = head_gain.astype(jnp.float32).reshape(HEADS, HDIM)
    causal = jnp.arange(CH)[:, None] >= jnp.arange(CH)[None, :]

    def block_step(carry_state, inputs):
        query_block, key_block, value_block = inputs
        query_f = query_block.astype(jnp.float32)
        key_f = key_block.astype(jnp.float32)
        value_f = value_block.astype(jnp.float32)
        scores = jnp.einsum('ishd,jshd->shij', query_f, key_f, precision=highest)
        weights = rounded(jnp.where(causal, scores, 0.0))
        within = jnp.einsum('shij,jshd->ishd', weights, value_f, precision=highest)
        across = jnp.einsum('ishd,shde->ishe', query_f, rounded(carry_state), precision=highest)
        mixed_sum = within + across
        inv_scale = lax.rsqrt(lax.optimization_barrier(jnp.mean(mixed_sum * mixed_sum, axis=-1, keepdims=True)) + epsilon)
        normed = (mixed_sum * inv_scale * head_gains).astype(jnp.bfloat16)
        carry_state = carry_state + jnp.einsum('jshd,jshe->shde', key_f, value_f, precision=highest)
        return (carry_state, normed)
    initial = jnp.zeros((SEQS, HEADS, HDIM, HDIM), jnp.float32)
    final_state, normed = lax.scan(block_step, initial, (query_blocks, key_blocks, value_blocks))
    attended = normed.reshape(LEN, SEQS, HEADS * HDIM).astype(jnp.float32)
    attn_proj = jnp.einsum('lsk,kd->lsd', attended, out_weight.astype(jnp.float32), precision=highest)
    stream = residual.astype(jnp.float32) + attn_proj
    inv_norm = lax.rsqrt(lax.optimization_barrier(jnp.mean(stream * stream, axis=-1, keepdims=True)) + epsilon)
    moe_in = (stream * inv_norm * norm_gain.astype(jnp.float32)).astype(jnp.bfloat16)
    tokens = moe_in.reshape(TOKENS, D)
    block_count = TOKENS // TOK_DEV
    route_ids = expert_ids.reshape(block_count, TOK_DEV * 2)
    one_hot = (route_ids[:, :, None] == jnp.arange(EXPERTS, dtype=jnp.int32)[None, None, :]).astype(jnp.int32)
    earlier = lax.optimization_barrier(jnp.sum((jnp.cumsum(one_hot, axis=1) - one_hot) * one_hot, axis=2))
    block_index = jnp.arange(block_count, dtype=jnp.int32)[:, None]
    per_expert = block_count * MOST
    buffer_index = (route_ids * per_expert + block_index * MOST + earlier).reshape(TOKENS * 2).astype(jnp.int32)
    dispatched = jnp.zeros((EXPERTS * per_expert, D), jnp.bfloat16).at[buffer_index].set(jnp.repeat(tokens, 2, axis=0))
    slice_width = FF // N_CTX

    def run_expert(inputs):
        rows_in, gate_part, up_part, down_part = inputs
        rows_f = rows_in.astype(jnp.float32)
        gate_act = jnp.einsum('rd,dcf->rcf', rows_f, gate_part.astype(jnp.float32).reshape(D, N_CTX, slice_width), precision=highest)
        up_act = jnp.einsum('rd,dcf->rcf', rows_f, up_part.astype(jnp.float32).reshape(D, N_CTX, slice_width), precision=highest)
        hidden = rounded(jax.nn.silu(gate_act) * up_act)
        part_sums = jnp.einsum('rcf,cfd->rcd', hidden, down_part.astype(jnp.float32).reshape(N_CTX, slice_width, D), precision=highest)
        return lax.optimization_barrier(jnp.sum(rounded(part_sums), axis=1)).astype(jnp.bfloat16)
    expert_y = lax.map(run_expert, (dispatched.reshape(EXPERTS, per_expert, D), gate_weight, up_weight, down_weight))
    picked = expert_y.reshape(EXPERTS * per_expert, D)[buffer_index].reshape(TOKENS, 2, D).astype(jnp.float32)
    moe_out = lax.optimization_barrier(jnp.sum(gate_weights.reshape(TOKENS, 2, 1) * picked, axis=1))
    return (stream.reshape(TOKENS, D) + moe_out).astype(jnp.bfloat16).reshape(LEN, SEQS, D)
```

```python
import jax
import jax.numpy as jnp
from jax import lax
from jax.sharding import Mesh, PartitionSpec as P

HDIM = 128
NX, NZ, NY, NC = 4, 8, 4, 2
CTX, EXP = ("x", "z"), ("y", "c")
EXPERTS = NY * NC
MOST = 6

epsilon = 1e-05
bf16, f32 = jnp.bfloat16, jnp.float32


def shift(block, axis, by):
    count = {"x": NX, "z": NZ}[axis]
    return lax.ppermute(block, axis, [(i, (i + by) % count) for i in range(count)])


def prior_sums(state):
    blocks = NX * NZ
    parts = state.astype(bf16).reshape(blocks, -1, HDIM)
    mine = lax.all_to_all(parts, CTX, split_axis=0, concat_axis=0, tiled=True)
    earlier = (jnp.arange(blocks)[:, None] > jnp.arange(blocks)[None, :]).astype(bf16)
    sums = lax.dot_general(
        earlier, mine, (((1,), (0,)), ((), ())), preferred_element_type=f32
    ).astype(bf16)
    back = lax.all_to_all(sums, CTX, split_axis=0, concat_axis=0, tiled=True)
    return back.reshape(state.shape)


def attend(queries, keys, values, prior, gains):
    scores = jnp.einsum("ishd,jshd->shij", queries, keys, preferred_element_type=f32)
    length = queries.shape[0]
    causal = jnp.arange(length)[:, None] >= jnp.arange(length)[None, :]
    weights = jnp.where(causal, scores, 0.0).astype(bf16)
    within = jnp.einsum("shij,jshd->ishd", weights, values, preferred_element_type=f32)
    across = jnp.einsum("ishd,shde->ishe", queries, prior, preferred_element_type=f32)
    mixed = within + across
    scale = lax.rsqrt(jnp.mean(mixed * mixed, axis=-1, keepdims=True) + epsilon)
    return (mixed * scale * gains).astype(bf16)


def cat(parts):
    return jnp.concatenate(parts, axis=0)


def gather_a(rows):
    ring = {0: rows}
    up = down = rows
    for k in range(1, 5):
        up = shift(up, "z", 1)
        ring[NZ - k] = up
        if k < 4:
            down = shift(down, "z", -1)
            ring[k] = down
    own = cat([ring[j] for j in range(NZ)])
    left, right = shift(own, "x", 1), shift(own, "x", -1)
    half = own.shape[0] // 2
    far = cat([shift(left[:half], "x", 1), shift(right[half:], "x", -1)])
    return own, right, far, left


def gather_b(rows):
    left, right, far = shift(rows, "x", 1), shift(rows, "x", -1), shift(rows, "x", 2)
    own = cat([rows, right, far, left])
    parts = {0: own}
    up = down = own
    for k in range(1, 4):
        up, down = shift(up, "z", 1), shift(down, "z", -1)
        parts[NZ - k], parts[k] = up, down
    half = own.shape[0] // 2
    parts[4] = cat([shift(up[:half], "z", 1), shift(down[half:], "z", -1)])
    return parts


def plus(one, *more):
    total = one.astype(f32)
    for other in more:
        total = total + other.astype(f32)
    return total.astype(bf16)


def scatter_a(own, right, far, left):
    half = own.shape[0] // 2
    to_right, to_left = shift(far[:half], "x", 1), shift(far[half:], "x", -1)
    right = cat([plus(right[:half], to_right), right[half:]])
    left = cat([left[:half], plus(left[half:], to_left)])
    total = plus(own, shift(right, "x", 1), shift(left, "x", -1))
    group = total.shape[0] // NZ
    ring = [total[j * group : (j + 1) * group] for j in range(NZ)]
    up = shift(ring[4], "z", 1)
    for j in (3, 2, 1):
        up = shift(plus(ring[j], up), "z", 1)
    down = shift(ring[5], "z", -1)
    for j in (6, 7):
        down = shift(plus(ring[j], down), "z", -1)
    return plus(ring[0], up, down)


def scatter_b(parts):
    half = parts[0].shape[0] // 2
    up, down = shift(parts[4][:half], "z", 1), shift(parts[4][half:], "z", -1)
    up = cat([plus(parts[3][:half], up), parts[3][half:]])
    down = cat([parts[5][:half], plus(parts[5][half:], down)])
    for k in (2, 1):
        up = plus(parts[k], shift(up, "z", 1))
        down = plus(parts[NZ - k], shift(down, "z", -1))
    total = plus(parts[0], shift(up, "z", 1), shift(down, "z", -1))
    group = total.shape[0] // NX
    own, right, far, left = [total[i * group : (i + 1) * group] for i in range(NX)]
    return plus(own, shift(right, "x", 1), shift(left, "x", -1), shift(far, "x", 2))


def local(
    queries,
    key_vecs,
    values,
    seq_lengths,
    head_gain,
    out_weight,
    residual,
    norm_gain,
    expert_ids,
    gate_weights,
    gate_weight,
    up_weight,
    down_weight,
):
    tok_rows, seq_count, head_width = queries.shape
    head_count = head_width // HDIM
    model_width = residual.shape[-1]
    query_heads = queries.reshape(tok_rows, seq_count, head_count, HDIM)
    key_heads = key_vecs.reshape(tok_rows, seq_count, head_count, HDIM)
    value_heads = values.reshape(tok_rows, seq_count, head_count, HDIM)
    position = lax.axis_index(CTX) * tok_rows + jnp.arange(tok_rows, dtype=jnp.int32)
    live_keys = position[:, None] < seq_lengths[None, :]
    key_heads = jnp.where(live_keys[:, :, None, None], key_heads, jnp.zeros_like(key_heads))
    head_gains = head_gain.astype(f32).reshape(head_count, HDIM)
    state = jnp.einsum("jshd,jshe->shde", key_heads, value_heads, preferred_element_type=f32)
    prior_state = prior_sums(state)
    normed = attend(query_heads, key_heads, value_heads, prior_state, head_gains)
    attended = normed.reshape(tok_rows, seq_count, head_width)
    projected = jnp.einsum(
        "rsk,kd->rsd", attended, out_weight, preferred_element_type=f32
    ).astype(bf16)
    pieces = lax.all_to_all(projected, EXP, split_axis=0, concat_axis=0, tiled=True)
    attn_proj = jnp.sum(pieces.reshape((EXPERTS,) + residual.shape).astype(f32), axis=0)
    stream = residual.astype(f32) + attn_proj
    inv_norm = lax.rsqrt(jnp.mean(stream * stream, axis=-1, keepdims=True) + epsilon)
    moe_in = (stream * inv_norm * norm_gain.astype(f32)).astype(bf16)
    tokens = moe_in.reshape(-1, model_width)
    tok_count = tokens.shape[0]
    total_rows = EXPERTS * MOST
    route_ids = expert_ids.reshape(tok_count * 2)
    order = jnp.arange(tok_count * 2)
    same = (route_ids[:, None] == route_ids[None, :]) & (order[:, None] > order[None, :])
    slots = (route_ids * MOST + jnp.sum(same.astype(jnp.int32), axis=1)).reshape(tok_count, 2)
    target = jnp.arange(total_rows, dtype=jnp.int32)
    hits = slots[:, :, None] == target[None, None, :]
    picker = jnp.sum(hits.astype(f32), axis=1).astype(bf16)
    blend = jnp.sum(
        gate_weights.reshape(tok_count, 2)[:, :, None] * hits.astype(f32), axis=1
    )
    outgoing = lax.dot_general(
        picker, tokens, (((0,), (0,)), ((), ())), preferred_element_type=f32
    ).astype(bf16)
    arrived = lax.all_to_all(outgoing, EXP, split_axis=0, concat_axis=0, tiled=True)

    def expert(rows):
        gate_act = jnp.dot(rows, gate_weight[0], preferred_element_type=f32)
        up_act = jnp.dot(rows, up_weight[0], preferred_element_type=f32)
        hidden = (jax.nn.silu(gate_act) * up_act).astype(bf16)
        return jnp.dot(hidden, down_weight[0], preferred_element_type=f32).astype(bf16)

    half = total_rows // 2
    a_parts = gather_a(arrived[:half])
    b_parts = gather_b(arrived[half:])
    a_sums = [expert(p) for p in a_parts]
    b_sums = {j: expert(p) for j, p in b_parts.items()}
    summed = cat([scatter_a(*a_sums), scatter_b(b_sums)])
    returned = lax.all_to_all(summed, EXP, split_axis=0, concat_axis=0, tiled=True)
    moe_out = jnp.dot(blend, returned.astype(f32), precision=lax.Precision.HIGHEST)
    return (stream + moe_out.reshape(stream.shape)).astype(bf16)


def solution(mesh):
    split = Mesh(mesh.devices.reshape(NX, NZ, NY, NC), CTX + EXP)
    each = P(CTX + EXP, None, None)
    return jax.shard_map(
        local,
        mesh=split,
        in_specs=(
            P(CTX, None, EXP),
            P(CTX, None, EXP),
            P(CTX, None, EXP),
            P(),
            P(EXP),
            P(EXP, None),
            each,
            P(),
            each,
            each,
            P(EXP, None, CTX),
            P(EXP, None, CTX),
            P(EXP, CTX, None),
        ),
        out_specs=each,
        check_vma=False,
    )
```

```python
import jax
import jax.numpy as jnp
from jax import lax
from jax.experimental import pallas as pl
from jax.experimental.pallas import tpu as pltpu
from jax.sharding import Mesh, PartitionSpec as P

HDIM = 128
NX, NZ, NY, NC = 4, 8, 4, 2
CTX, EXP = ("x", "z"), ("y", "c")
EXPERTS = NY * NC
MOST = 6

epsilon = 1e-05
bf16, f32 = jnp.bfloat16, jnp.float32


def shift(block, axis, by):
    count = {"x": NX, "z": NZ}[axis]
    return lax.ppermute(block, axis, [(i, (i + by) % count) for i in range(count)])


def prior_sums(state):
    blocks = NX * NZ
    parts = state.astype(bf16).reshape(blocks, -1, HDIM)
    mine = lax.all_to_all(parts, CTX, split_axis=0, concat_axis=0, tiled=True)
    earlier = (jnp.arange(blocks)[:, None] > jnp.arange(blocks)[None, :]).astype(bf16)
    sums = lax.dot_general(
        earlier, mine, (((1,), (0,)), ((), ())), preferred_element_type=f32
    ).astype(bf16)
    back = lax.all_to_all(sums, CTX, split_axis=0, concat_axis=0, tiled=True)
    return back.reshape(state.shape)


def attend(queries, keys, values, prior, gains):
    scores = jnp.einsum("ishd,jshd->shij", queries, keys, preferred_element_type=f32)
    length = queries.shape[0]
    causal = jnp.arange(length)[:, None] >= jnp.arange(length)[None, :]
    weights = jnp.where(causal, scores, 0.0).astype(bf16)
    within = jnp.einsum("shij,jshd->ishd", weights, values, preferred_element_type=f32)
    across = jnp.einsum("ishd,shde->ishe", queries, prior, preferred_element_type=f32)
    mixed = within + across
    scale = lax.rsqrt(jnp.mean(mixed * mixed, axis=-1, keepdims=True) + epsilon)
    return (mixed * scale * gains).astype(bf16)


def stack(parts):
    rows = [p.shape[0] for p in parts]

    def body(*refs):
        *sources, out, sems = refs
        copies = [
            pltpu.make_async_copy(src, out.at[pl.ds(sum(rows[:i]), rows[i])], sems.at[i])
            for i, src in enumerate(sources)
        ]
        for copy in copies:
            copy.start()
        for copy in copies:
            copy.wait()

    return pl.pallas_call(
        body,
        out_shape=jax.ShapeDtypeStruct((sum(rows), parts[0].shape[1]), parts[0].dtype),
        in_specs=[pl.BlockSpec(memory_space=pltpu.HBM)] * len(parts),
        out_specs=pl.BlockSpec(memory_space=pltpu.HBM),
        scratch_shapes=[pltpu.SemaphoreType.DMA((len(parts),))],
        cost_estimate=pl.CostEstimate(
            flops=0, bytes_accessed=4 * sum(rows) * parts[0].shape[1], transcendentals=0
        ),
    )(*parts)


NT = (((1,), (1,)), ((), ()))


def expert(blocks, gate_t, up_t, down, at_once):
    width, hidden = gate_t.shape[1], gate_t.shape[0]
    tall = [b.shape[0] for b in blocks]
    total = sum(tall)
    chunk = min(at_once, *tall)
    pieces = [(i, r) for i, rows in enumerate(tall) for r in range(0, rows, chunk)]
    steps = total // at_once
    wide = 512

    def body(*refs):
        n = len(blocks)
        ins, weights, outs = refs[:n], refs[n : n + 3], refs[n + 3 : 2 * n + 3]
        x, y, wg, wu, wd, in_sem, out_sem, w_sem = refs[2 * n + 3 :]
        loads = [
            pltpu.make_async_copy(
                ins[i].at[pl.ds(r, chunk)], x.at[pl.ds(k * chunk, chunk)], in_sem.at[k]
            )
            for k, (i, r) in enumerate(pieces)
        ]
        stores = [
            pltpu.make_async_copy(
                y.at[pl.ds(k * chunk, chunk)], outs[i].at[pl.ds(r, chunk)], out_sem.at[k]
            )
            for k, (i, r) in enumerate(pieces)
        ]
        fetch = [
            pltpu.make_async_copy(src, dst, w_sem.at[k])
            for k, (src, dst) in enumerate(zip(weights, (wg, wu, wd)))
        ]
        each = at_once // chunk
        fetch[0].start()
        for load in loads[:each]:
            load.start()
        fetch[1].start()
        fetch[2].start()
        for load in loads[each:]:
            load.start()
        for s in range(steps):
            for load in loads[s * each : (s + 1) * each]:
                load.wait()
            rows = pl.ds(s * at_once, at_once)
            if s == 0:
                fetch[0].wait()
            gate = lax.dot_general(x[rows, :], wg[...], NT, preferred_element_type=f32)
            if s == 0:
                fetch[1].wait()
            up = lax.dot_general(x[rows, :], wu[...], NT, preferred_element_type=f32)
            acts = (gate / (1.0 + jnp.exp(-gate)) * up).astype(bf16)
            if s == 0:
                fetch[2].wait()
            for c in range(0, width, wide):
                y[rows, pl.ds(c, wide)] = jnp.dot(
                    acts, wd[:, pl.ds(c, wide)], preferred_element_type=f32
                ).astype(bf16)
            for store in stores[s * each : (s + 1) * each]:
                store.start()
        for store in stores:
            store.wait()

    return pl.pallas_call(
        body,
        out_shape=[jax.ShapeDtypeStruct(b.shape, bf16) for b in blocks],
        in_specs=[pl.BlockSpec(memory_space=pltpu.HBM)] * (len(blocks) + 3),
        out_specs=[pl.BlockSpec(memory_space=pltpu.HBM)] * len(blocks),
        scratch_shapes=[
            pltpu.VMEM((total, width), bf16),
            pltpu.VMEM((total, width), bf16),
            pltpu.VMEM((hidden, width), bf16),
            pltpu.VMEM((hidden, width), bf16),
            pltpu.VMEM((hidden, width), bf16),
            pltpu.SemaphoreType.DMA((len(pieces),)),
            pltpu.SemaphoreType.DMA((len(pieces),)),
            pltpu.SemaphoreType.DMA((3,)),
        ],
        compiler_params=pltpu.CompilerParams(vmem_limit_bytes=40 * 2**20),
        cost_estimate=pl.CostEstimate(
            flops=6 * total * width * hidden,
            bytes_accessed=4 * total * width + 6 * hidden * width,
            transcendentals=total * hidden,
        ),
    )(*blocks, gate_t, up_t, down)


def plus(one, *more):
    total = one.astype(f32)
    for other in more:
        total = total + other.astype(f32)
    return total.astype(bf16)


def after(value, *others):
    return lax.optimization_barrier((value, *others))[0]


def scatter_both(near, far, b_sums):
    low, high, left_low, left_high, right_low, right_high = near
    far_low, far_high = far
    right_low = plus(right_low, shift(far_low, "x", 1))
    left_high = plus(left_high, shift(far_high, "x", -1))
    high = plus(high, shift(right_high, "x", 1), shift(left_high, "x", -1))
    low = plus(low, shift(left_low, "x", -1), shift(right_low, "x", 1))
    group = low.shape[0] // 4
    ring = [half[j * group : (j + 1) * group] for half in (low, high) for j in range(4)]
    up, down = shift(ring[4], "z", 1), shift(ring[5], "z", -1)
    for j in (3, 2):
        up, down = plus(ring[j], up), plus(ring[9 - j], down)
        up, down = shift(up, "z", 1), shift(down, "z", -1)
    up = plus(ring[1], up)
    b_sums = lax.psum_scatter(b_sums, "z", scatter_dimension=0, tiled=True)
    b_sums = scatter_x_small(after(b_sums, up))
    return jnp.concatenate([plus(ring[0], shift(up, "z", 1), down), b_sums], axis=0)


def gather_both(a_rows, b_rows):
    up, down = shift(a_rows, "z", 1), shift(a_rows, "z", -1)
    beside = [shift(b_rows, "x", by) for by in (-1, 2, 1)]
    b_all = lax.all_gather(
        stack([b_rows] + after(beside, up, down)), "z", axis=0, tiled=True
    )
    ring = {0: a_rows, NZ - 1: up, 1: down}
    for k in range(2, 5):
        up = shift(up, "z", 1)
        ring[NZ - k] = up
        if k < 4:
            down = shift(down, "z", -1)
            ring[k] = down
    low, high = stack([ring[j] for j in range(4)]), stack([ring[j] for j in range(4, NZ)])
    moved = [shift(part, "x", by) for by in (1, -1) for part in (low, high)]
    left_low, left_high, right_low, right_high = lax.optimization_barrier(moved)
    far = [shift(left_low, "x", 1), shift(right_high, "x", -1)]
    return (low, high, left_low, left_high, right_low, right_high), far, b_all


def scatter_x_small(total):
    group = total.shape[0] // NX
    own, right, far, left = [total[i * group : (i + 1) * group] for i in range(NX)]
    return plus(own, shift(right, "x", 1), shift(left, "x", -1), shift(far, "x", 2))


def local(
    queries,
    key_vecs,
    values,
    seq_lengths,
    head_gain,
    out_weight,
    residual,
    norm_gain,
    expert_ids,
    gate_weights,
    gate_weight,
    up_weight,
    down_weight,
):
    tok_rows, seq_count, head_width = queries.shape
    head_count = head_width // HDIM
    model_width = residual.shape[-1]
    query_heads = queries.reshape(tok_rows, seq_count, head_count, HDIM)
    key_heads = key_vecs.reshape(tok_rows, seq_count, head_count, HDIM)
    value_heads = values.reshape(tok_rows, seq_count, head_count, HDIM)
    position = lax.axis_index(CTX) * tok_rows + jnp.arange(tok_rows, dtype=jnp.int32)
    live_keys = position[:, None] < seq_lengths[None, :]
    key_heads = jnp.where(live_keys[:, :, None, None], key_heads, jnp.zeros_like(key_heads))
    head_gains = head_gain.astype(f32).reshape(head_count, HDIM)
    state = jnp.einsum("jshd,jshe->shde", key_heads, value_heads, preferred_element_type=f32)
    prior_state = prior_sums(state)
    normed = attend(query_heads, key_heads, value_heads, prior_state, head_gains)
    attended = normed.reshape(tok_rows, seq_count, head_width)
    projected = jnp.einsum(
        "rsk,kd->rsd", attended, out_weight, preferred_element_type=f32
    ).astype(bf16)
    pieces = lax.all_to_all(projected, EXP, split_axis=0, concat_axis=0, tiled=True)
    attn_proj = jnp.sum(pieces.reshape((EXPERTS,) + residual.shape).astype(f32), axis=0)
    stream = residual.astype(f32) + attn_proj
    inv_norm = lax.rsqrt(jnp.mean(stream * stream, axis=-1, keepdims=True) + epsilon)
    moe_in = (stream * inv_norm * norm_gain.astype(f32)).astype(bf16)
    tokens = moe_in.reshape(-1, model_width)
    tok_count = tokens.shape[0]
    total_rows = EXPERTS * MOST
    route_ids = expert_ids.reshape(tok_count * 2)
    order = jnp.arange(tok_count * 2)
    same = (route_ids[:, None] == route_ids[None, :]) & (order[:, None] > order[None, :])
    slots = (route_ids * MOST + jnp.sum(same.astype(jnp.int32), axis=1)).reshape(tok_count, 2)
    target = jnp.arange(total_rows, dtype=jnp.int32)
    hits = slots[:, :, None] == target[None, None, :]
    picker = jnp.sum(hits.astype(f32), axis=1).astype(bf16)
    blend = jnp.sum(
        gate_weights.reshape(tok_count, 2)[:, :, None] * hits.astype(f32), axis=1
    )
    outgoing = lax.dot_general(
        picker, tokens, (((0,), (0,)), ((), ())), preferred_element_type=f32
    ).astype(bf16)
    arrived = lax.all_to_all(outgoing, EXP, split_axis=0, concat_axis=0, tiled=True)

    weights = (gate_weight[0].T, up_weight[0].T, down_weight[0])
    half = total_rows // 2
    near, far, b_rows = gather_both(arrived[:half], arrived[half:])
    near = expert(near, *weights, 192)
    far = expert(after(far, *near), *weights, 192)
    (b_sums,) = expert([after(b_rows, *near, *far)], *weights, 256)
    summed = scatter_both(near, far, b_sums)
    returned = lax.all_to_all(summed, EXP, split_axis=0, concat_axis=0, tiled=True)
    moe_out = jnp.dot(blend, returned.astype(f32), precision=lax.Precision.HIGHEST)
    return (stream + moe_out.reshape(stream.shape)).astype(bf16)


def solution(mesh):
    split = Mesh(mesh.devices.reshape(NX, NZ, NY, NC), CTX + EXP)
    each = P(CTX + EXP, None, None)
    return jax.shard_map(
        local,
        mesh=split,
        in_specs=(
            P(CTX, None, EXP),
            P(CTX, None, EXP),
            P(CTX, None, EXP),
            P(),
            P(EXP),
            P(EXP, None),
            each,
            P(),
            each,
            each,
            P(EXP, None, CTX),
            P(EXP, None, CTX),
            P(EXP, CTX, None),
        ),
        out_specs=each,
        check_vma=False,
    )
```

```python
import jax
import jax.numpy as jnp
from jax import lax
from jax.experimental import pallas as pl
from jax.experimental.pallas import tpu as pltpu
from jax.sharding import Mesh, PartitionSpec as P

HDIM = 128
NX, NZ, NY, NC = 4, 8, 4, 2
CTX, EXP = ("x", "z"), ("y", "c")
EXPERTS = NY * NC
MOST = 6

epsilon = 1e-05
bf16, f32 = jnp.bfloat16, jnp.float32


def shift(block, axis, by):
    count = {"x": NX, "z": NZ}[axis]
    return lax.ppermute(block, axis, [(i, (i + by) % count) for i in range(count)])


def prior_sums(state):
    blocks = NX * NZ
    parts = state.astype(bf16).reshape(blocks, -1, HDIM)
    mine = lax.all_to_all(parts, CTX, split_axis=0, concat_axis=0, tiled=True)
    earlier = (jnp.arange(blocks)[:, None] > jnp.arange(blocks)[None, :]).astype(bf16)
    sums = lax.dot_general(
        earlier, mine, (((1,), (0,)), ((), ())), preferred_element_type=f32
    ).astype(bf16)
    back = lax.all_to_all(sums, CTX, split_axis=0, concat_axis=0, tiled=True)
    return back.reshape(state.shape)


def attend(queries, keys, values, prior, gains):
    scores = jnp.einsum("ishd,jshd->shij", queries, keys, preferred_element_type=f32)
    length = queries.shape[0]
    causal = jnp.arange(length)[:, None] >= jnp.arange(length)[None, :]
    weights = jnp.where(causal, scores, 0.0).astype(bf16)
    within = jnp.einsum("shij,jshd->ishd", weights, values, preferred_element_type=f32)
    across = jnp.einsum("ishd,shde->ishe", queries, prior, preferred_element_type=f32)
    mixed = within + across
    scale = lax.rsqrt(jnp.mean(mixed * mixed, axis=-1, keepdims=True) + epsilon)
    return (mixed * scale * gains).astype(bf16)


HBM = pl.BlockSpec(memory_space=pltpu.HBM)


def in_hbm(*arrays):
    return [pltpu.with_memory_space_constraint(x, pltpu.HBM) for x in arrays]


def stack(parts, *before):
    rows = [p.shape[0] for p in parts]
    shape = (sum(rows), parts[0].shape[1])

    def body(*refs):
        out, sems = refs[-2:]
        copies = [
            pltpu.make_async_copy(refs[i], out.at[pl.ds(sum(rows[:i]), rows[i])], sems.at[i])
            for i in range(len(rows))
        ]
        for copy in copies:
            copy.start()
        for copy in copies:
            copy.wait()

    return pl.pallas_call(
        body,
        out_shape=jax.ShapeDtypeStruct(shape, parts[0].dtype),
        in_specs=[HBM] * (len(parts) + len(before)),
        out_specs=pl.BlockSpec(memory_space=pltpu.VMEM),
        scratch_shapes=[pltpu.SemaphoreType.DMA((len(parts),))],
        compiler_params=pltpu.CompilerParams(vmem_limit_bytes=8 * 2**20),
        cost_estimate=pl.CostEstimate(
            flops=0, bytes_accessed=4 * shape[0] * shape[1], transcendentals=0
        ),
    )(*parts, *before)


NT = (((1,), (1,)), ((), ()))


def expert(blocks, gate_t, up_t, down, at_once, *before):
    width, hidden = gate_t.shape[1], gate_t.shape[0]
    tall = [b.shape[0] for b in blocks]
    total = sum(tall)
    chunk = min(at_once, *tall)
    pieces = [(i, r) for i, rows in enumerate(tall) for r in range(0, rows, chunk)]
    steps = total // at_once
    wide = 512

    def body(*refs):
        n = len(blocks)
        ins, weights, outs = refs[:n], refs[n : n + 3], refs[-n - 8 : -8]
        x, y, wg, wu, wd, in_sem, out_sem, w_sem = refs[-8:]
        loads = [
            pltpu.make_async_copy(
                ins[i].at[pl.ds(r, chunk)], x.at[pl.ds(k * chunk, chunk)], in_sem.at[k]
            )
            for k, (i, r) in enumerate(pieces)
        ]
        stores = [
            pltpu.make_async_copy(
                y.at[pl.ds(k * chunk, chunk)], outs[i].at[pl.ds(r, chunk)], out_sem.at[k]
            )
            for k, (i, r) in enumerate(pieces)
        ]
        fetch = [
            pltpu.make_async_copy(src, dst, w_sem.at[k])
            for k, (src, dst) in enumerate(zip(weights, (wg, wu, wd)))
        ]
        each = at_once // chunk
        fetch[0].start()
        for load in loads[:each]:
            load.start()
        fetch[1].start()
        fetch[2].start()
        for load in loads[each:]:
            load.start()
        for s in range(steps):
            for load in loads[s * each : (s + 1) * each]:
                load.wait()
            rows = pl.ds(s * at_once, at_once)
            if s == 0:
                fetch[0].wait()
            gate = lax.dot_general(x[rows, :], wg[...], NT, preferred_element_type=f32)
            if s == 0:
                fetch[1].wait()
            up = lax.dot_general(x[rows, :], wu[...], NT, preferred_element_type=f32)
            acts = (gate / (1.0 + jnp.exp(-gate)) * up).astype(bf16)
            if s == 0:
                fetch[2].wait()
            for c in range(0, width, wide):
                y[rows, pl.ds(c, wide)] = jnp.dot(
                    acts, wd[:, pl.ds(c, wide)], preferred_element_type=f32
                ).astype(bf16)
            for store in stores[s * each : (s + 1) * each]:
                store.start()
        for store in stores:
            store.wait()

    return pl.pallas_call(
        body,
        out_shape=[pltpu.HBM(b.shape, bf16) for b in blocks],
        in_specs=[HBM] * (len(blocks) + 3 + len(before)),
        out_specs=[HBM] * len(blocks),
        scratch_shapes=[
            pltpu.VMEM((total, width), bf16),
            pltpu.VMEM((total, width), bf16),
            pltpu.VMEM((hidden, width), bf16),
            pltpu.VMEM((hidden, width), bf16),
            pltpu.VMEM((hidden, width), bf16),
            pltpu.SemaphoreType.DMA((len(pieces),)),
            pltpu.SemaphoreType.DMA((len(pieces),)),
            pltpu.SemaphoreType.DMA((3,)),
        ],
        compiler_params=pltpu.CompilerParams(vmem_limit_bytes=24 * 2**20),
        cost_estimate=pl.CostEstimate(
            flops=6 * total * width * hidden,
            bytes_accessed=4 * total * width + 6 * hidden * width,
            transcendentals=total * hidden,
        ),
    )(*blocks, *in_hbm(gate_t, up_t, down), *before)


def plus(one, *more):
    total = one.astype(f32)
    for other in more:
        total = total + other.astype(f32)
    return total.astype(bf16)


def scatter_both(near, far, b_sums):
    low, high, left_low, left_high, right_low, right_high = near
    far_low, far_high = far
    right_low = plus(right_low, shift(far_low, "x", 1))
    left_high = plus(left_high, shift(far_high, "x", -1))
    high = plus(high, shift(right_high, "x", 1), shift(left_high, "x", -1))
    low = plus(low, shift(left_low, "x", -1), shift(right_low, "x", 1))
    group = low.shape[0] // 4
    parts = [half[j * group : (j + 1) * group] for half in (low, high) for j in range(4)]
    a_sums = plus(parts[0], *[shift(parts[j], "z", j) for j in (4, 3, 5, 2, 6, 1, 7)])
    b_sums = scatter_x_small(lax.psum_scatter(b_sums, "z", scatter_dimension=0, tiled=True))
    return jnp.concatenate([a_sums, b_sums], axis=0)


def gather_both(a_rows, b_rows):
    beside = [shift(b_rows, "x", by) for by in (-1, 2, 1)]
    along = {j: shift(a_rows, "z", -j) for j in (4, 3, 5, 2, 6, 1, 7)}
    along[0] = a_rows
    b_all = lax.all_gather(stack([b_rows] + beside, along[1], along[7]), "z", axis=0, tiled=True)
    low, high = stack([along[j] for j in range(4)]), stack([along[j] for j in range(4, NZ)])
    moved = [shift(part, "x", by) for by in (1, -1) for part in (low, high)]
    left_low, left_high, right_low, right_high = lax.optimization_barrier(moved)
    far = [shift(left_low, "x", 1), shift(right_high, "x", -1)]
    return (low, high, left_low, left_high, right_low, right_high), far, b_all


def scatter_x_small(total):
    group = total.shape[0] // NX
    own, right, far, left = [total[i * group : (i + 1) * group] for i in range(NX)]
    return plus(own, shift(right, "x", 1), shift(left, "x", -1), shift(far, "x", 2))


def local(
    queries,
    key_vecs,
    values,
    seq_lengths,
    head_gain,
    out_weight,
    residual,
    norm_gain,
    expert_ids,
    gate_weights,
    gate_weight,
    up_weight,
    down_weight,
):
    tok_rows, seq_count, head_width = queries.shape
    head_count = head_width // HDIM
    model_width = residual.shape[-1]
    query_heads = queries.reshape(tok_rows, seq_count, head_count, HDIM)
    key_heads = key_vecs.reshape(tok_rows, seq_count, head_count, HDIM)
    value_heads = values.reshape(tok_rows, seq_count, head_count, HDIM)
    position = lax.axis_index(CTX) * tok_rows + jnp.arange(tok_rows, dtype=jnp.int32)
    live_keys = position[:, None] < seq_lengths[None, :]
    key_heads = jnp.where(live_keys[:, :, None, None], key_heads, jnp.zeros_like(key_heads))
    head_gains = head_gain.astype(f32).reshape(head_count, HDIM)
    state = jnp.einsum("jshd,jshe->shde", key_heads, value_heads, preferred_element_type=f32)
    prior_state = prior_sums(state)
    normed = attend(query_heads, key_heads, value_heads, prior_state, head_gains)
    attended = normed.reshape(tok_rows, seq_count, head_width)
    projected = jnp.einsum(
        "rsk,kd->rsd", attended, out_weight, preferred_element_type=f32
    ).astype(bf16)
    pieces = lax.all_to_all(projected, EXP, split_axis=0, concat_axis=0, tiled=True)
    attn_proj = jnp.sum(pieces.reshape((EXPERTS,) + residual.shape).astype(f32), axis=0)
    stream = residual.astype(f32) + attn_proj
    inv_norm = lax.rsqrt(jnp.mean(stream * stream, axis=-1, keepdims=True) + epsilon)
    moe_in = (stream * inv_norm * norm_gain.astype(f32)).astype(bf16)
    tokens = moe_in.reshape(-1, model_width)
    tok_count = tokens.shape[0]
    total_rows = EXPERTS * MOST
    route_ids = expert_ids.reshape(tok_count * 2)
    order = jnp.arange(tok_count * 2)
    same = (route_ids[:, None] == route_ids[None, :]) & (order[:, None] > order[None, :])
    slots = (route_ids * MOST + jnp.sum(same.astype(jnp.int32), axis=1)).reshape(tok_count, 2)
    target = jnp.arange(total_rows, dtype=jnp.int32)
    hits = slots[:, :, None] == target[None, None, :]
    picker = jnp.sum(hits.astype(f32), axis=1).astype(bf16)
    blend = jnp.sum(
        gate_weights.reshape(tok_count, 2)[:, :, None] * hits.astype(f32), axis=1
    )
    outgoing = lax.dot_general(
        picker, tokens, (((0,), (0,)), ((), ())), preferred_element_type=f32
    ).astype(bf16)
    arrived = lax.all_to_all(outgoing, EXP, split_axis=0, concat_axis=0, tiled=True)

    weights = (gate_weight[0].T, up_weight[0].T, down_weight[0])
    half = total_rows // 2
    near, far, b_rows = gather_both(arrived[:half], arrived[half:])
    near = expert(near, *weights, 192)
    (b_sums,) = expert(in_hbm(b_rows), *weights, 256, *in_hbm(near[0]), *far)
    far = expert(far, *weights, 192, *in_hbm(b_sums))
    summed = scatter_both(near, far, b_sums)
    returned = lax.all_to_all(summed, EXP, split_axis=0, concat_axis=0, tiled=True)
    moe_out = jnp.dot(blend, returned.astype(f32), precision=lax.Precision.HIGHEST)
    return (stream + moe_out.reshape(stream.shape)).astype(bf16)


def solution(mesh):
    split = Mesh(mesh.devices.reshape(NX, NZ, NY, NC), CTX + EXP)
    each = P(CTX + EXP, None, None)
    return jax.shard_map(
        local,
        mesh=split,
        in_specs=(
            P(CTX, None, EXP),
            P(CTX, None, EXP),
            P(CTX, None, EXP),
            P(),
            P(EXP),
            P(EXP, None),
            each,
            P(),
            each,
            each,
            P(EXP, None, CTX),
            P(EXP, None, CTX),
            P(EXP, CTX, None),
        ),
        out_specs=each,
        check_vma=False,
    )
```

```python
import jax
import jax.numpy as jnp
from jax import lax
from jax.experimental import pallas as pl
from jax.experimental.pallas import tpu as pltpu
from jax.sharding import Mesh, PartitionSpec as P

HDIM = 128
NX, NZ, NY, NC = 4, 8, 4, 2
CTX, EXP = ("x", "z"), ("y", "c")
EXPERTS = NY * NC
MOST = 6

epsilon = 1e-05
bf16, f32 = jnp.bfloat16, jnp.float32


def shift(block, axis, by):
    count = {"x": NX, "z": NZ}[axis]
    return lax.ppermute(block, axis, [(i, (i + by) % count) for i in range(count)])


def prior_sums(state):
    blocks = NX * NZ
    parts = state.astype(bf16).reshape(blocks, -1, HDIM)
    mine = lax.all_to_all(parts, CTX, split_axis=0, concat_axis=0, tiled=True)
    earlier = (jnp.arange(blocks)[:, None] > jnp.arange(blocks)[None, :]).astype(bf16)
    sums = lax.dot_general(
        earlier, mine, (((1,), (0,)), ((), ())), preferred_element_type=f32
    ).astype(bf16)
    back = lax.all_to_all(sums, CTX, split_axis=0, concat_axis=0, tiled=True)
    return back.reshape(state.shape)


def attend(queries, keys, values, prior, gains):
    scores = jnp.einsum("ishd,jshd->shij", queries, keys, preferred_element_type=f32)
    length = queries.shape[0]
    causal = jnp.arange(length)[:, None] >= jnp.arange(length)[None, :]
    weights = jnp.where(causal, scores, 0.0).astype(bf16)
    within = jnp.einsum("shij,jshd->ishd", weights, values, preferred_element_type=f32)
    across = jnp.einsum("ishd,shde->ishe", queries, prior, preferred_element_type=f32)
    mixed = within + across
    scale = lax.rsqrt(jnp.mean(mixed * mixed, axis=-1, keepdims=True) + epsilon)
    return (mixed * scale * gains).astype(bf16)


HBM = pl.BlockSpec(memory_space=pltpu.HBM)


def in_hbm(*arrays):
    return [pltpu.with_memory_space_constraint(x, pltpu.HBM) for x in arrays]


def stack(parts, *before):
    rows, width = parts[0].shape

    def body(*refs):
        out, sems = refs[-2:]
        copies = [
            pltpu.make_async_copy(refs[i], out.at[i], sems.at[i]) for i in range(len(parts))
        ]
        for copy in copies:
            copy.start()
        for copy in copies:
            copy.wait()

    whole = pl.pallas_call(
        body,
        out_shape=jax.ShapeDtypeStruct((len(parts), rows, width), parts[0].dtype),
        in_specs=[HBM] * (len(parts) + len(before)),
        out_specs=pl.BlockSpec(memory_space=pltpu.VMEM),
        scratch_shapes=[pltpu.SemaphoreType.DMA((len(parts),))],
        compiler_params=pltpu.CompilerParams(vmem_limit_bytes=8 * 2**20),
        cost_estimate=pl.CostEstimate(
            flops=0, bytes_accessed=4 * len(parts) * rows * width, transcendentals=0
        ),
    )(*parts, *before)
    return whole.reshape(-1, width)


NT = (((1,), (1,)), ((), ()))


def expert(blocks, gate_t, up_t, down, at_once, *before):
    width, hidden = gate_t.shape[1], gate_t.shape[0]
    tall = [b.shape[0] for b in blocks]
    total = sum(tall)
    chunk = min(at_once, *tall)
    pieces = [(i, r) for i, rows in enumerate(tall) for r in range(0, rows, chunk)]
    steps = total // at_once
    wide = 512

    def body(*refs):
        n = len(blocks)
        ins, weights, outs = refs[:n], refs[n : n + 3], refs[-n - 8 : -8]
        x, y, wg, wu, wd, in_sem, out_sem, w_sem = refs[-8:]
        loads = [
            pltpu.make_async_copy(
                ins[i].at[pl.ds(r, chunk)], x.at[pl.ds(k * chunk, chunk)], in_sem.at[k]
            )
            for k, (i, r) in enumerate(pieces)
        ]
        stores = [
            pltpu.make_async_copy(
                y.at[pl.ds(k * chunk, chunk)], outs[i].at[pl.ds(r, chunk)], out_sem.at[k]
            )
            for k, (i, r) in enumerate(pieces)
        ]
        fetch = [
            pltpu.make_async_copy(src, dst, w_sem.at[k])
            for k, (src, dst) in enumerate(zip(weights, (wg, wu, wd)))
        ]
        each = at_once // chunk
        fetch[0].start()
        for load in loads[:each]:
            load.start()
        fetch[1].start()
        fetch[2].start()
        for load in loads[each:]:
            load.start()
        for s in range(steps):
            for load in loads[s * each : (s + 1) * each]:
                load.wait()
            rows = pl.ds(s * at_once, at_once)
            if s == 0:
                fetch[0].wait()
            gate = lax.dot_general(x[rows, :], wg[...], NT, preferred_element_type=f32)
            if s == 0:
                fetch[1].wait()
            up = lax.dot_general(x[rows, :], wu[...], NT, preferred_element_type=f32)
            acts = (gate / (1.0 + jnp.exp(-gate)) * up).astype(bf16)
            if s == 0:
                fetch[2].wait()
            for c in range(0, width, wide):
                y[rows, pl.ds(c, wide)] = jnp.dot(
                    acts, wd[:, pl.ds(c, wide)], preferred_element_type=f32
                ).astype(bf16)
            for store in stores[s * each : (s + 1) * each]:
                store.start()
        for store in stores:
            store.wait()

    return pl.pallas_call(
        body,
        out_shape=[pltpu.HBM(b.shape, bf16) for b in blocks],
        in_specs=[HBM] * (len(blocks) + 3 + len(before)),
        out_specs=[HBM] * len(blocks),
        scratch_shapes=[
            pltpu.VMEM((total, width), bf16),
            pltpu.VMEM((total, width), bf16),
            pltpu.VMEM((hidden, width), bf16),
            pltpu.VMEM((hidden, width), bf16),
            pltpu.VMEM((hidden, width), bf16),
            pltpu.SemaphoreType.DMA((len(pieces),)),
            pltpu.SemaphoreType.DMA((len(pieces),)),
            pltpu.SemaphoreType.DMA((3,)),
        ],
        compiler_params=pltpu.CompilerParams(vmem_limit_bytes=24 * 2**20),
        cost_estimate=pl.CostEstimate(
            flops=6 * total * width * hidden,
            bytes_accessed=4 * total * width + 6 * hidden * width,
            transcendentals=total * hidden,
        ),
    )(*blocks, *in_hbm(gate_t, up_t, down), *before)


def plus(one, *more):
    total = one.astype(f32)
    for other in more:
        total = total + other.astype(f32)
    return total.astype(bf16)


def scatter_both(near, far, b1, b2):
    low, high, left_low, left_high, right_low, right_high = near
    far_low, far_high = far
    b1 = lax.psum_scatter(b1, "z", scatter_dimension=0, tiled=True)
    right_low = plus(right_low, shift(far_low, "x", 1))
    left_high = plus(left_high, shift(far_high, "x", -1))
    high = plus(high, shift(right_high, "x", 1), shift(left_high, "x", -1))
    low = plus(low, shift(left_low, "x", -1), shift(right_low, "x", 1))
    group = low.shape[0] // 4
    parts = [half[j * group : (j + 1) * group] for half in (low, high) for j in range(4)]
    a_sums = plus(parts[0], *[shift(parts[j], "z", j) for j in (4, 3, 5, 2, 6, 1, 7)])
    b1, b2 = lax.optimization_barrier((b1, b2))
    b2 = lax.psum_scatter(b2, "z", scatter_dimension=0, tiled=True)
    return jnp.concatenate([a_sums, scatter_x(b1), scatter_x(b2)], axis=0)


def scatter_x(total):
    group = total.shape[0] // NX
    own, right, far, left = [total[i * group : (i + 1) * group] for i in range(NX)]
    return plus(own, shift(right, "x", 1), shift(left, "x", -1), shift(far, "x", 2))


def gather_both(a_rows, b_rows):
    up, down = shift(a_rows, "z", 1), shift(a_rows, "z", -1)
    b_all = []
    for rows in b_rows:
        beside = [rows] + [shift(rows, "x", by) for by in (-1, 2, 1)]
        own = stack(beside, up, down) if not b_all else stack(beside)
        b_all.append(lax.all_gather(own, "z", axis=0, tiled=True))
    ring = {0: a_rows, NZ - 1: up, 1: down}
    for k in range(2, 5):
        up = shift(up, "z", 1)
        ring[NZ - k] = up
        if k < 4:
            down = shift(down, "z", -1)
            ring[k] = down
    low, high = stack([ring[j] for j in range(4)]), stack([ring[j] for j in range(4, NZ)])
    moved = [shift(part, "x", by) for by in (1, -1) for part in (low, high)]
    left_low, left_high, right_low, right_high = lax.optimization_barrier(moved)
    far = [shift(left_low, "x", 1), shift(right_high, "x", -1)]
    return (low, high, left_low, left_high, right_low, right_high), far, b_all


def local(
    queries,
    key_vecs,
    values,
    seq_lengths,
    head_gain,
    out_weight,
    residual,
    norm_gain,
    expert_ids,
    gate_weights,
    gate_weight,
    up_weight,
    down_weight,
):
    tok_rows, seq_count, head_width = queries.shape
    head_count = head_width // HDIM
    model_width = residual.shape[-1]
    query_heads = queries.reshape(tok_rows, seq_count, head_count, HDIM)
    key_heads = key_vecs.reshape(tok_rows, seq_count, head_count, HDIM)
    value_heads = values.reshape(tok_rows, seq_count, head_count, HDIM)
    position = lax.axis_index(CTX) * tok_rows + jnp.arange(tok_rows, dtype=jnp.int32)
    live_keys = position[:, None] < seq_lengths[None, :]
    key_heads = jnp.where(live_keys[:, :, None, None], key_heads, jnp.zeros_like(key_heads))
    head_gains = head_gain.astype(f32).reshape(head_count, HDIM)
    state = jnp.einsum("jshd,jshe->shde", key_heads, value_heads, preferred_element_type=f32)
    prior_state = prior_sums(state)
    normed = attend(query_heads, key_heads, value_heads, prior_state, head_gains)
    attended = normed.reshape(tok_rows, seq_count, head_width)
    projected = jnp.einsum(
        "rsk,kd->rsd", attended, out_weight, preferred_element_type=f32
    ).astype(bf16)
    pieces = lax.all_to_all(projected, EXP, split_axis=0, concat_axis=0, tiled=True)
    attn_proj = jnp.sum(pieces.reshape((EXPERTS,) + residual.shape).astype(f32), axis=0)
    stream = residual.astype(f32) + attn_proj
    inv_norm = lax.rsqrt(jnp.mean(stream * stream, axis=-1, keepdims=True) + epsilon)
    moe_in = (stream * inv_norm * norm_gain.astype(f32)).astype(bf16)
    tokens = moe_in.reshape(-1, model_width)
    tok_count = tokens.shape[0]
    total_rows = EXPERTS * MOST
    route_ids = expert_ids.reshape(tok_count * 2)
    order = jnp.arange(tok_count * 2)
    same = (route_ids[:, None] == route_ids[None, :]) & (order[:, None] > order[None, :])
    slots = (route_ids * MOST + jnp.sum(same.astype(jnp.int32), axis=1)).reshape(tok_count, 2)
    target = jnp.arange(total_rows, dtype=jnp.int32)
    hits = slots[:, :, None] == target[None, None, :]
    picker = jnp.sum(hits.astype(f32), axis=1).astype(bf16)
    blend = jnp.sum(
        gate_weights.reshape(tok_count, 2)[:, :, None] * hits.astype(f32), axis=1
    )
    outgoing = lax.dot_general(
        picker, tokens, (((0,), (0,)), ((), ())), preferred_element_type=f32
    ).astype(bf16)
    arrived = lax.all_to_all(outgoing, EXP, split_axis=0, concat_axis=0, tiled=True)

    weights = (gate_weight[0].T, up_weight[0].T, down_weight[0])
    cut = (total_rows // 2, total_rows - 8)
    near, far, (b1, b2) = gather_both(
        arrived[: cut[0]], (arrived[cut[0] : cut[1]], arrived[cut[1] :])
    )
    near = expert(near, *weights, 288)
    (b1,) = expert(in_hbm(b1), *weights, 256, *in_hbm(near[0]), *far)
    far = expert(far, *weights, 192, *in_hbm(b1))
    (b2,) = expert(in_hbm(b2), *weights, 256, *in_hbm(far[0]))
    summed = scatter_both(near, far, b1, b2)
    returned = lax.all_to_all(summed, EXP, split_axis=0, concat_axis=0, tiled=True)
    moe_out = jnp.dot(blend, returned.astype(f32), precision=lax.Precision.HIGHEST)
    return (stream + moe_out.reshape(stream.shape)).astype(bf16)


def solution(mesh):
    split = Mesh(mesh.devices.reshape(NX, NZ, NY, NC), CTX + EXP)
    each = P(CTX + EXP, None, None)
    return jax.shard_map(
        local,
        mesh=split,
        in_specs=(
            P(CTX, None, EXP),
            P(CTX, None, EXP),
            P(CTX, None, EXP),
            P(),
            P(EXP),
            P(EXP, None),
            each,
            P(),
            each,
            each,
            P(EXP, None, CTX),
            P(EXP, None, CTX),
            P(EXP, CTX, None),
        ),
        out_specs=each,
        check_vma=False,
    )
```

```python
import math

import jax
import jax.numpy as jnp
from jax import lax
from jax.experimental import pallas as pl
from jax.experimental.pallas import tpu as pltpu
from jax.sharding import Mesh, PartitionSpec as P

HDIM = 128
NX, NZ, NY, NC = 4, 8, 4, 2
CTX, EXP = ("x", "z"), ("y", "c")
EXPERTS = NY * NC
MOST = 6

epsilon = 1e-05
bf16, f32 = jnp.bfloat16, jnp.float32


def shift(block, axis, by):
    count = {"x": NX, "z": NZ}[axis]
    return lax.ppermute(block, axis, [(i, (i + by) % count) for i in range(count)])


def prior_sums(state):
    blocks = NX * NZ
    parts = state.astype(bf16).reshape(blocks, -1, HDIM)
    mine = lax.all_to_all(parts, CTX, split_axis=0, concat_axis=0, tiled=True)
    earlier = (jnp.arange(blocks)[:, None] > jnp.arange(blocks)[None, :]).astype(bf16)
    sums = lax.dot_general(
        earlier, mine, (((1,), (0,)), ((), ())), preferred_element_type=f32
    ).astype(bf16)
    back = lax.all_to_all(sums, CTX, split_axis=0, concat_axis=0, tiled=True)
    return back.reshape(state.shape)


def attend(queries, keys, values, prior, gains):
    scores = jnp.einsum("ishd,jshd->shij", queries, keys, preferred_element_type=f32)
    length = queries.shape[0]
    causal = jnp.arange(length)[:, None] >= jnp.arange(length)[None, :]
    weights = jnp.where(causal, scores, 0.0).astype(bf16)
    within = jnp.einsum("shij,jshd->ishd", weights, values, preferred_element_type=f32)
    across = jnp.einsum("ishd,shde->ishe", queries, prior, preferred_element_type=f32)
    mixed = within + across
    scale = lax.rsqrt(jnp.mean(mixed * mixed, axis=-1, keepdims=True) + epsilon)
    return (mixed * scale * gains).astype(bf16)


HBM = pl.BlockSpec(memory_space=pltpu.HBM)


def in_hbm(*arrays):
    return [pltpu.with_memory_space_constraint(x, pltpu.HBM) for x in arrays]


def stack(parts, *before):
    rows, width = parts[0].shape

    def body(*refs):
        out, sems = refs[-2:]
        copies = [
            pltpu.make_async_copy(refs[i], out.at[i], sems.at[i]) for i in range(len(parts))
        ]
        for copy in copies:
            copy.start()
        for copy in copies:
            copy.wait()

    whole = pl.pallas_call(
        body,
        out_shape=jax.ShapeDtypeStruct((len(parts), rows, width), parts[0].dtype),
        in_specs=[HBM] * (len(parts) + len(before)),
        out_specs=pl.BlockSpec(memory_space=pltpu.VMEM),
        scratch_shapes=[pltpu.SemaphoreType.DMA((len(parts),))],
        compiler_params=pltpu.CompilerParams(vmem_limit_bytes=8 * 2**20),
        cost_estimate=pl.CostEstimate(
            flops=0, bytes_accessed=4 * len(parts) * rows * width, transcendentals=0
        ),
    )(*parts, *before)
    return whole.reshape(-1, width)


NT = (((1,), (1,)), ((), ()))


def expert(blocks, gate_t, up_t, down, at_once, *before):
    width, hidden = gate_t.shape[1], gate_t.shape[0]
    tall = [b.shape[0] for b in blocks]
    total = sum(tall)
    chunk = math.gcd(at_once, *tall)
    pieces = [(i, r) for i, rows in enumerate(tall) for r in range(0, rows, chunk)]
    steps = total // at_once
    wide = 512

    def body(*refs):
        n = len(blocks)
        ins, weights, outs = refs[:n], refs[n : n + 3], refs[-n - 8 : -8]
        x, y, wg, wu, wd, in_sem, out_sem, w_sem = refs[-8:]
        loads = [
            pltpu.make_async_copy(
                ins[i].at[pl.ds(r, chunk)], x.at[pl.ds(k * chunk, chunk)], in_sem.at[k]
            )
            for k, (i, r) in enumerate(pieces)
        ]
        stores = [
            pltpu.make_async_copy(
                y.at[pl.ds(k * chunk, chunk)], outs[i].at[pl.ds(r, chunk)], out_sem.at[k]
            )
            for k, (i, r) in enumerate(pieces)
        ]
        fetch = [
            pltpu.make_async_copy(src, dst, w_sem.at[k])
            for k, (src, dst) in enumerate(zip(weights, (wg, wu, wd)))
        ]
        each = at_once // chunk
        fetch[0].start()
        for load in loads[:each]:
            load.start()
        fetch[1].start()
        fetch[2].start()
        for load in loads[each:]:
            load.start()
        for s in range(steps):
            for load in loads[s * each : (s + 1) * each]:
                load.wait()
            rows = pl.ds(s * at_once, at_once)
            if s == 0:
                fetch[0].wait()
            gate = lax.dot_general(x[rows, :], wg[...], NT, preferred_element_type=f32)
            if s == 0:
                fetch[1].wait()
            up = lax.dot_general(x[rows, :], wu[...], NT, preferred_element_type=f32)
            acts = (gate / (1.0 + jnp.exp(-gate)) * up).astype(bf16)
            if s == 0:
                fetch[2].wait()
            for c in range(0, width, wide):
                y[rows, pl.ds(c, wide)] = jnp.dot(
                    acts, wd[:, pl.ds(c, wide)], preferred_element_type=f32
                ).astype(bf16)
            for store in stores[s * each : (s + 1) * each]:
                store.start()
        for store in stores:
            store.wait()

    return pl.pallas_call(
        body,
        out_shape=[pltpu.HBM(b.shape, bf16) for b in blocks],
        in_specs=[HBM] * (len(blocks) + 3 + len(before)),
        out_specs=[HBM] * len(blocks),
        scratch_shapes=[
            pltpu.VMEM((total, width), bf16),
            pltpu.VMEM((total, width), bf16),
            pltpu.VMEM((hidden, width), bf16),
            pltpu.VMEM((hidden, width), bf16),
            pltpu.VMEM((hidden, width), bf16),
            pltpu.SemaphoreType.DMA((len(pieces),)),
            pltpu.SemaphoreType.DMA((len(pieces),)),
            pltpu.SemaphoreType.DMA((3,)),
        ],
        compiler_params=pltpu.CompilerParams(vmem_limit_bytes=24 * 2**20),
        cost_estimate=pl.CostEstimate(
            flops=6 * total * width * hidden,
            bytes_accessed=4 * total * width + 6 * hidden * width,
            transcendentals=total * hidden,
        ),
    )(*blocks, *in_hbm(gate_t, up_t, down), *before)


def plus(one, *more):
    total = one.astype(f32)
    for other in more:
        total = total + other.astype(f32)
    return total.astype(bf16)


PIECES = ((0, 1, 7), (2, 6), (3, 4, 5))


def gather_a(rows):
    ring = {0: rows}
    up = down = rows
    for k in range(1, 5):
        up = shift(up, "z", 1)
        ring[NZ - k] = up
        if k < 4:
            down = shift(down, "z", -1)
            ring[k] = down
    own = [stack([ring[j] for j in piece]) for piece in PIECES]
    left = [shift(piece, "x", 1) for piece in own]
    right = [shift(piece, "x", -1) for piece in own]
    far = [shift(left[0], "x", 1), shift(left[1], "x", 1), shift(right[2], "x", -1)]
    return own, left, right, far


def scatter_a(own, left, right, far):
    left, right = list(left), list(right)
    left[2] = plus(left[2], shift(far[2], "x", -1))
    right[1] = plus(right[1], shift(far[1], "x", 1))
    right[0] = plus(right[0], shift(far[0], "x", 1))
    at = {}
    for q in (2, 1, 0):
        total = plus(own[q], shift(right[q], "x", 1), shift(left[q], "x", -1))
        group = total.shape[0] // len(PIECES[q])
        for i, j in enumerate(PIECES[q]):
            at[j] = total[i * group : (i + 1) * group]
    up, down = shift(at[4], "z", 1), shift(at[5], "z", -1)
    for j in (3, 2, 1):
        up = shift(plus(at[j], up), "z", 1)
        if j > 1:
            down = shift(plus(at[9 - j], down), "z", -1)
    return plus(at[0], up, down)


def gather_b(rows, *before):
    own = stack([rows] + [shift(rows, "x", by) for by in (-1, 2, 1)], *before)
    return lax.all_gather(own, "z", axis=0, tiled=True)


def scatter_b(sums):
    total = lax.psum_scatter(sums, "z", scatter_dimension=0, tiled=True)
    group = total.shape[0] // NX
    own, right, far, left = [total[i * group : (i + 1) * group] for i in range(NX)]
    return plus(own, shift(right, "x", 1), shift(left, "x", -1), shift(far, "x", 2))


def local(
    queries,
    key_vecs,
    values,
    seq_lengths,
    head_gain,
    out_weight,
    residual,
    norm_gain,
    expert_ids,
    gate_weights,
    gate_weight,
    up_weight,
    down_weight,
):
    tok_rows, seq_count, head_width = queries.shape
    head_count = head_width // HDIM
    model_width = residual.shape[-1]
    query_heads = queries.reshape(tok_rows, seq_count, head_count, HDIM)
    key_heads = key_vecs.reshape(tok_rows, seq_count, head_count, HDIM)
    value_heads = values.reshape(tok_rows, seq_count, head_count, HDIM)
    position = lax.axis_index(CTX) * tok_rows + jnp.arange(tok_rows, dtype=jnp.int32)
    live_keys = position[:, None] < seq_lengths[None, :]
    key_heads = jnp.where(live_keys[:, :, None, None], key_heads, jnp.zeros_like(key_heads))
    head_gains = head_gain.astype(f32).reshape(head_count, HDIM)
    state = jnp.einsum("jshd,jshe->shde", key_heads, value_heads, preferred_element_type=f32)
    prior_state = prior_sums(state)
    normed = attend(query_heads, key_heads, value_heads, prior_state, head_gains)
    attended = normed.reshape(tok_rows, seq_count, head_width)
    projected = jnp.einsum(
        "rsk,kd->rsd", attended, out_weight, preferred_element_type=f32
    ).astype(bf16)
    pieces = lax.all_to_all(projected, EXP, split_axis=0, concat_axis=0, tiled=True)
    attn_proj = jnp.sum(pieces.reshape((EXPERTS,) + residual.shape).astype(f32), axis=0)
    stream = residual.astype(f32) + attn_proj
    inv_norm = lax.rsqrt(jnp.mean(stream * stream, axis=-1, keepdims=True) + epsilon)
    moe_in = (stream * inv_norm * norm_gain.astype(f32)).astype(bf16)
    tokens = moe_in.reshape(-1, model_width)
    tok_count = tokens.shape[0]
    total_rows = EXPERTS * MOST
    route_ids = expert_ids.reshape(tok_count * 2)
    order = jnp.arange(tok_count * 2)
    same = (route_ids[:, None] == route_ids[None, :]) & (order[:, None] > order[None, :])
    slots = (route_ids * MOST + jnp.sum(same.astype(jnp.int32), axis=1)).reshape(tok_count, 2)
    target = jnp.arange(total_rows, dtype=jnp.int32)
    hits = slots[:, :, None] == target[None, None, :]
    picker = jnp.sum(hits.astype(f32), axis=1).astype(bf16)
    blend = jnp.sum(
        gate_weights.reshape(tok_count, 2)[:, :, None] * hits.astype(f32), axis=1
    )
    outgoing = lax.dot_general(
        picker, tokens, (((0,), (0,)), ((), ())), preferred_element_type=f32
    ).astype(bf16)
    arrived = lax.all_to_all(outgoing, EXP, split_axis=0, concat_axis=0, tiled=True)

    weights = (gate_weight[0].T, up_weight[0].T, down_weight[0])
    cut = total_rows * 2 // 3
    own, left, right, far = gather_a(arrived[:cut])
    b_rows = gather_b(arrived[cut:], own[0])
    early = expert(own + left[:2] + right[:2], *weights, 288)
    late = expert(far + left[2:] + right[2:], *weights, 224, *in_hbm(early[0]))
    (b_sums,) = expert(in_hbm(b_rows), *weights, 256, *in_hbm(late[0]))
    a_sums = scatter_a(early[:3], early[3:5] + late[3:4], early[5:7] + late[4:5], late[:3])
    summed = jnp.concatenate([a_sums, scatter_b(b_sums)], axis=0)
    returned = lax.all_to_all(summed, EXP, split_axis=0, concat_axis=0, tiled=True)
    moe_out = jnp.dot(blend, returned.astype(f32), precision=lax.Precision.HIGHEST)
    return (stream + moe_out.reshape(stream.shape)).astype(bf16)


def solution(mesh):
    split = Mesh(mesh.devices.reshape(NX, NZ, NY, NC), CTX + EXP)
    each = P(CTX + EXP, None, None)
    return jax.shard_map(
        local,
        mesh=split,
        in_specs=(
            P(CTX, None, EXP),
            P(CTX, None, EXP),
            P(CTX, None, EXP),
            P(),
            P(EXP),
            P(EXP, None),
            each,
            P(),
            each,
            each,
            P(EXP, None, CTX),
            P(EXP, None, CTX),
            P(EXP, CTX, None),
        ),
        out_specs=each,
        check_vma=False,
    )
```

```python
import math

import jax
import jax.numpy as jnp
from jax import lax
from jax.experimental import pallas as pl
from jax.experimental.pallas import tpu as pltpu
from jax.sharding import Mesh, PartitionSpec as P

HDIM = 128
NX, NZ, NY, NC = 4, 8, 4, 2
CTX, EXP = ("x", "z"), ("y", "c")
EXPERTS = NY * NC
MOST = 6

epsilon = 1e-05
bf16, f32 = jnp.bfloat16, jnp.float32


def shift(block, axis, by):
    count = {"x": NX, "z": NZ}[axis]
    return lax.ppermute(block, axis, [(i, (i + by) % count) for i in range(count)])


def prior_sums(state):
    blocks = NX * NZ
    parts = state.astype(bf16).reshape(blocks, -1, HDIM)
    mine = lax.all_to_all(parts, CTX, split_axis=0, concat_axis=0, tiled=True)
    earlier = (jnp.arange(blocks)[:, None] > jnp.arange(blocks)[None, :]).astype(bf16)
    sums = lax.dot_general(
        earlier, mine, (((1,), (0,)), ((), ())), preferred_element_type=f32
    ).astype(bf16)
    back = lax.all_to_all(sums, CTX, split_axis=0, concat_axis=0, tiled=True)
    return back.reshape(state.shape)


def attend(queries, keys, values, prior, gains):
    scores = jnp.einsum("ishd,jshd->shij", queries, keys, preferred_element_type=f32)
    length = queries.shape[0]
    causal = jnp.arange(length)[:, None] >= jnp.arange(length)[None, :]
    weights = jnp.where(causal, scores, 0.0).astype(bf16)
    within = jnp.einsum("shij,jshd->ishd", weights, values, preferred_element_type=f32)
    across = jnp.einsum("ishd,shde->ishe", queries, prior, preferred_element_type=f32)
    mixed = within + across
    scale = lax.rsqrt(jnp.mean(mixed * mixed, axis=-1, keepdims=True) + epsilon)
    return (mixed * scale * gains).astype(bf16)


HBM = pl.BlockSpec(memory_space=pltpu.HBM)


def in_hbm(*arrays):
    return [pltpu.with_memory_space_constraint(x, pltpu.HBM) for x in arrays]


def stack(parts, *before):
    rows, width = parts[0].shape

    def body(*refs):
        out, sems = refs[-2:]
        copies = [
            pltpu.make_async_copy(refs[i], out.at[i], sems.at[i]) for i in range(len(parts))
        ]
        for copy in copies:
            copy.start()
        for copy in copies:
            copy.wait()

    whole = pl.pallas_call(
        body,
        out_shape=jax.ShapeDtypeStruct((len(parts), rows, width), parts[0].dtype),
        in_specs=[HBM] * (len(parts) + len(before)),
        out_specs=pl.BlockSpec(memory_space=pltpu.VMEM),
        scratch_shapes=[pltpu.SemaphoreType.DMA((len(parts),))],
        compiler_params=pltpu.CompilerParams(vmem_limit_bytes=8 * 2**20),
        cost_estimate=pl.CostEstimate(
            flops=0, bytes_accessed=4 * len(parts) * rows * width, transcendentals=0
        ),
    )(*parts, *before)
    return whole.reshape(-1, width)


NT = (((1,), (1,)), ((), ()))


def expert(blocks, gate_t, up_t, down, at_once, *before):
    width, hidden = gate_t.shape[1], gate_t.shape[0]
    tall = [b.shape[0] for b in blocks]
    total = sum(tall)
    chunk = math.gcd(at_once, *tall)
    pieces = [(i, r) for i, rows in enumerate(tall) for r in range(0, rows, chunk)]
    steps = total // at_once
    wide = 512

    def body(*refs):
        n = len(blocks)
        ins, weights, outs = refs[:n], refs[n : n + 3], refs[-n - 8 : -8]
        x, y, wg, wu, wd, in_sem, out_sem, w_sem = refs[-8:]
        loads = [
            pltpu.make_async_copy(
                ins[i].at[pl.ds(r, chunk)], x.at[pl.ds(k * chunk, chunk)], in_sem.at[k]
            )
            for k, (i, r) in enumerate(pieces)
        ]
        stores = [
            pltpu.make_async_copy(
                y.at[pl.ds(k * chunk, chunk)], outs[i].at[pl.ds(r, chunk)], out_sem.at[k]
            )
            for k, (i, r) in enumerate(pieces)
        ]
        fetch = [
            pltpu.make_async_copy(src, dst, w_sem.at[k])
            for k, (src, dst) in enumerate(zip(weights, (wg, wu, wd)))
        ]
        each = at_once // chunk
        fetch[0].start()
        for load in loads[:each]:
            load.start()
        fetch[1].start()
        fetch[2].start()
        for load in loads[each:]:
            load.start()
        for s in range(steps):
            for load in loads[s * each : (s + 1) * each]:
                load.wait()
            rows = pl.ds(s * at_once, at_once)
            if s == 0:
                fetch[0].wait()
            gate = lax.dot_general(x[rows, :], wg[...], NT, preferred_element_type=f32)
            if s == 0:
                fetch[1].wait()
            up = lax.dot_general(x[rows, :], wu[...], NT, preferred_element_type=f32)
            acts = (gate / (1.0 + jnp.exp(-gate)) * up).astype(bf16)
            if s == 0:
                fetch[2].wait()
            for c in range(0, width, wide):
                y[rows, pl.ds(c, wide)] = jnp.dot(
                    acts, wd[:, pl.ds(c, wide)], preferred_element_type=f32
                ).astype(bf16)
            for store in stores[s * each : (s + 1) * each]:
                store.start()
        for store in stores:
            store.wait()

    return pl.pallas_call(
        body,
        out_shape=[pltpu.HBM(b.shape, bf16) for b in blocks],
        in_specs=[HBM] * (len(blocks) + 3 + len(before)),
        out_specs=[HBM] * len(blocks),
        scratch_shapes=[
            pltpu.VMEM((total, width), bf16),
            pltpu.VMEM((total, width), bf16),
            pltpu.VMEM((hidden, width), bf16),
            pltpu.VMEM((hidden, width), bf16),
            pltpu.VMEM((hidden, width), bf16),
            pltpu.SemaphoreType.DMA((len(pieces),)),
            pltpu.SemaphoreType.DMA((len(pieces),)),
            pltpu.SemaphoreType.DMA((3,)),
        ],
        compiler_params=pltpu.CompilerParams(vmem_limit_bytes=24 * 2**20),
        cost_estimate=pl.CostEstimate(
            flops=6 * total * width * hidden,
            bytes_accessed=4 * total * width + 6 * hidden * width,
            transcendentals=total * hidden,
        ),
    )(*blocks, *in_hbm(gate_t, up_t, down), *before)


def plus(one, *more):
    total = one.astype(f32)
    for other in more:
        total = total + other.astype(f32)
    return total.astype(bf16)


PIECES = ((0, 1, 7), (2, 6), (3, 4, 5))


def gather_a(rows):
    ring = {0: rows}
    up = down = rows
    for k in range(1, 5):
        up = shift(up, "z", 1)
        ring[NZ - k] = up
        if k < 4:
            down = shift(down, "z", -1)
            ring[k] = down
    own, left, right = [], [], []
    for piece in PIECES:
        own.append(stack([ring[j] for j in piece], *left[-1:], *right[-1:]))
        left.append(shift(own[-1], "x", 1))
        right.append(shift(own[-1], "x", -1))
    far = [shift(left[0], "x", 1), shift(left[1], "x", 1), shift(right[2], "x", -1)]
    return own, left, right, far


def scatter_a(own, left, right, far, other):
    left, right = list(left), list(right)
    back = shift(far[2], "x", -1)
    back, left[0], left[1] = lax.optimization_barrier((back, left[0], left[1]))
    left[2] = plus(left[2], back)
    right[1] = plus(right[1], shift(far[1], "x", 1))
    right[0] = plus(right[0], shift(far[0], "x", 1))
    at = {}
    for q in (2, 1, 0):
        total = plus(own[q], shift(right[q], "x", 1), shift(left[q], "x", -1))
        if q == 2:
            total, other = lax.optimization_barrier((total, other))
        group = total.shape[0] // len(PIECES[q])
        for i, j in enumerate(PIECES[q]):
            at[j] = total[i * group : (i + 1) * group]
    up, down = shift(at[4], "z", 1), shift(at[5], "z", -1)
    for j in (3, 2, 1):
        up = shift(plus(at[j], up), "z", 1)
        if j > 1:
            down = shift(plus(at[9 - j], down), "z", -1)
    return plus(at[0], up, down), other


def gather_b(rows, *before):
    own = stack([rows] + [shift(rows, "x", by) for by in (-1, 2, 1)], *before)
    return lax.all_gather(own, "z", axis=0, tiled=True)


def scatter_x(total):
    group = total.shape[0] // NX
    own, right, far, left = [total[i * group : (i + 1) * group] for i in range(NX)]
    return plus(own, shift(right, "x", 1), shift(left, "x", -1), shift(far, "x", 2))


def local(
    queries,
    key_vecs,
    values,
    seq_lengths,
    head_gain,
    out_weight,
    residual,
    norm_gain,
    expert_ids,
    gate_weights,
    gate_weight,
    up_weight,
    down_weight,
):
    tok_rows, seq_count, head_width = queries.shape
    head_count = head_width // HDIM
    model_width = residual.shape[-1]
    query_heads = queries.reshape(tok_rows, seq_count, head_count, HDIM)
    key_heads = key_vecs.reshape(tok_rows, seq_count, head_count, HDIM)
    value_heads = values.reshape(tok_rows, seq_count, head_count, HDIM)
    position = lax.axis_index(CTX) * tok_rows + jnp.arange(tok_rows, dtype=jnp.int32)
    live_keys = position[:, None] < seq_lengths[None, :]
    key_heads = jnp.where(live_keys[:, :, None, None], key_heads, jnp.zeros_like(key_heads))
    head_gains = head_gain.astype(f32).reshape(head_count, HDIM)
    state = jnp.einsum("jshd,jshe->shde", key_heads, value_heads, preferred_element_type=f32)
    prior_state = prior_sums(state)
    normed = attend(query_heads, key_heads, value_heads, prior_state, head_gains)
    attended = normed.reshape(tok_rows, seq_count, head_width)
    projected = jnp.einsum(
        "rsk,kd->rsd", attended, out_weight, preferred_element_type=f32
    ).astype(bf16)
    pieces = lax.all_to_all(projected, EXP, split_axis=0, concat_axis=0, tiled=True)
    attn_proj = jnp.sum(pieces.reshape((EXPERTS,) + residual.shape).astype(f32), axis=0)
    stream = residual.astype(f32) + attn_proj
    inv_norm = lax.rsqrt(jnp.mean(stream * stream, axis=-1, keepdims=True) + epsilon)
    moe_in = (stream * inv_norm * norm_gain.astype(f32)).astype(bf16)
    tokens = moe_in.reshape(-1, model_width)
    tok_count = tokens.shape[0]
    total_rows = EXPERTS * MOST
    route_ids = expert_ids.reshape(tok_count * 2)
    order = jnp.arange(tok_count * 2)
    same = (route_ids[:, None] == route_ids[None, :]) & (order[:, None] > order[None, :])
    slots = (route_ids * MOST + jnp.sum(same.astype(jnp.int32), axis=1)).reshape(tok_count, 2)
    target = jnp.arange(total_rows, dtype=jnp.int32)
    hits = slots[:, :, None] == target[None, None, :]
    picker = jnp.sum(hits.astype(f32), axis=1).astype(bf16)
    blend = jnp.sum(
        gate_weights.reshape(tok_count, 2)[:, :, None] * hits.astype(f32), axis=1
    )
    outgoing = lax.dot_general(
        picker, tokens, (((0,), (0,)), ((), ())), preferred_element_type=f32
    ).astype(bf16)
    arrived = lax.all_to_all(outgoing, EXP, split_axis=0, concat_axis=0, tiled=True)

    weights = (gate_weight[0].T, up_weight[0].T, down_weight[0])
    cut = total_rows * 2 // 3
    own, left, right, far = gather_a(arrived[:cut])
    b_rows = gather_b(arrived[cut:], own[0])
    early = expert(own + left[:2] + right[:2], *weights, 288, right[2])
    (b_sums,) = expert(in_hbm(b_rows), *weights, 256, *in_hbm(early[0]), *far, left[2])
    late = expert(far + left[2:] + right[2:], *weights, 224, *in_hbm(b_sums))
    b_sums = lax.psum_scatter(b_sums, "z", scatter_dimension=0, tiled=True)
    a_sums, b_sums = scatter_a(
        early[:3], early[3:5] + late[3:4], early[5:7] + late[4:5], late[:3], b_sums
    )
    summed = jnp.concatenate([a_sums, scatter_x(b_sums)], axis=0)
    returned = lax.all_to_all(summed, EXP, split_axis=0, concat_axis=0, tiled=True)
    moe_out = jnp.dot(blend, returned.astype(f32), precision=lax.Precision.HIGHEST)
    return (stream + moe_out.reshape(stream.shape)).astype(bf16)


def solution(mesh):
    split = Mesh(mesh.devices.reshape(NX, NZ, NY, NC), CTX + EXP)
    each = P(CTX + EXP, None, None)
    return jax.shard_map(
        local,
        mesh=split,
        in_specs=(
            P(CTX, None, EXP),
            P(CTX, None, EXP),
            P(CTX, None, EXP),
            P(),
            P(EXP),
            P(EXP, None),
            each,
            P(),
            each,
            each,
            P(EXP, None, CTX),
            P(EXP, None, CTX),
            P(EXP, CTX, None),
        ),
        out_specs=each,
        check_vma=False,
    )
```

```python
import math

import jax
import jax.numpy as jnp
from jax import lax
from jax.experimental import pallas as pl
from jax.experimental.pallas import tpu as pltpu
from jax.sharding import Mesh, PartitionSpec as P

HDIM = 128
NX, NZ, NY, NC = 4, 8, 4, 2
CTX, EXP = ("x", "z"), ("y", "c")
EXPERTS = NY * NC
MOST = 6

epsilon = 1e-05
bf16, f32 = jnp.bfloat16, jnp.float32


def shift(block, axis, by):
    count = {"x": NX, "z": NZ}[axis]
    return lax.ppermute(block, axis, [(i, (i + by) % count) for i in range(count)])


def prior_sums(state):
    blocks = NX * NZ
    parts = state.astype(bf16).reshape(blocks, -1, HDIM)
    mine = lax.all_to_all(parts, CTX, split_axis=0, concat_axis=0, tiled=True)
    earlier = (jnp.arange(blocks)[:, None] > jnp.arange(blocks)[None, :]).astype(bf16)
    sums = lax.dot_general(
        earlier, mine, (((1,), (0,)), ((), ())), preferred_element_type=f32
    ).astype(bf16)
    back = lax.all_to_all(sums, CTX, split_axis=0, concat_axis=0, tiled=True)
    return back.reshape(state.shape)


def attend(queries, keys, values, prior, gains):
    scores = jnp.einsum("ishd,jshd->shij", queries, keys, preferred_element_type=f32)
    length = queries.shape[0]
    causal = jnp.arange(length)[:, None] >= jnp.arange(length)[None, :]
    weights = jnp.where(causal, scores, 0.0).astype(bf16)
    within = jnp.einsum("shij,jshd->ishd", weights, values, preferred_element_type=f32)
    across = jnp.einsum("ishd,shde->ishe", queries, prior, preferred_element_type=f32)
    mixed = within + across
    scale = lax.rsqrt(jnp.mean(mixed * mixed, axis=-1, keepdims=True) + epsilon)
    return (mixed * scale * gains).astype(bf16)


HBM = pl.BlockSpec(memory_space=pltpu.HBM)


def in_hbm(*arrays):
    return [pltpu.with_memory_space_constraint(x, pltpu.HBM) for x in arrays]


def stack(parts, *before):
    rows, width = parts[0].shape

    def body(*refs):
        out, sems = refs[-2:]
        copies = [
            pltpu.make_async_copy(refs[i], out.at[i], sems.at[i]) for i in range(len(parts))
        ]
        for copy in copies:
            copy.start()
        for copy in copies:
            copy.wait()

    whole = pl.pallas_call(
        body,
        out_shape=jax.ShapeDtypeStruct((len(parts), rows, width), parts[0].dtype),
        in_specs=[HBM] * (len(parts) + len(before)),
        out_specs=pl.BlockSpec(memory_space=pltpu.VMEM),
        scratch_shapes=[pltpu.SemaphoreType.DMA((len(parts),))],
        compiler_params=pltpu.CompilerParams(vmem_limit_bytes=8 * 2**20),
        cost_estimate=pl.CostEstimate(
            flops=0, bytes_accessed=4 * len(parts) * rows * width, transcendentals=0
        ),
    )(*parts, *before)
    return whole.reshape(-1, width)


NT = (((1,), (1,)), ((), ()))


def expert(blocks, gate_t, up_t, down, at_once, *before):
    width, hidden = gate_t.shape[1], gate_t.shape[0]
    tall = [b.shape[0] for b in blocks]
    total = sum(tall)
    chunk = math.gcd(at_once, *tall)
    pieces = [(i, r) for i, rows in enumerate(tall) for r in range(0, rows, chunk)]
    steps = total // at_once
    wide = 512
    second = -(-hidden // 128) * 128

    def body(*refs):
        n = len(blocks)
        ins, weights, outs = refs[:n], refs[n : n + 3], refs[-n - 7 : -7]
        x, y, wgu, wd, in_sem, out_sem, w_sem = refs[-7:]
        places = (wgu.at[pl.ds(0, hidden)], wgu.at[pl.ds(second, hidden)], wd)
        loads = [
            pltpu.make_async_copy(
                ins[i].at[pl.ds(r, chunk)], x.at[pl.ds(k * chunk, chunk)], in_sem.at[k]
            )
            for k, (i, r) in enumerate(pieces)
        ]
        stores = [
            pltpu.make_async_copy(
                y.at[pl.ds(k * chunk, chunk)], outs[i].at[pl.ds(r, chunk)], out_sem.at[k]
            )
            for k, (i, r) in enumerate(pieces)
        ]
        fetch = [
            pltpu.make_async_copy(src, dst, w_sem.at[k])
            for k, (src, dst) in enumerate(zip(weights, places))
        ]
        each = at_once // chunk
        fetch[0].start()
        wgu[pl.ds(hidden, second - hidden), :] = jnp.zeros((second - hidden, width), bf16)
        for load in loads[:each]:
            load.start()
        fetch[1].start()
        fetch[2].start()
        for load in loads[each:]:
            load.start()
        for s in range(steps):
            for load in loads[s * each : (s + 1) * each]:
                load.wait()
            rows = pl.ds(s * at_once, at_once)
            if s == 0:
                fetch[0].wait()
                fetch[1].wait()
            both = lax.dot_general(x[rows, :], wgu[...], NT, preferred_element_type=f32)
            gate, up = both[:, :hidden], both[:, second:]
            acts = (gate / (1.0 + jnp.exp(-gate)) * up).astype(bf16)
            if s == 0:
                fetch[2].wait()
            for c in range(0, width, wide):
                y[rows, pl.ds(c, wide)] = jnp.dot(
                    acts, wd[:, pl.ds(c, wide)], preferred_element_type=f32
                ).astype(bf16)
            for store in stores[s * each : (s + 1) * each]:
                store.start()
        for store in stores:
            store.wait()

    return pl.pallas_call(
        body,
        out_shape=[pltpu.HBM(b.shape, bf16) for b in blocks],
        in_specs=[HBM] * (len(blocks) + 3 + len(before)),
        out_specs=[HBM] * len(blocks),
        scratch_shapes=[
            pltpu.VMEM((total, width), bf16),
            pltpu.VMEM((total, width), bf16),
            pltpu.VMEM((second + hidden, width), bf16),
            pltpu.VMEM((hidden, width), bf16),
            pltpu.SemaphoreType.DMA((len(pieces),)),
            pltpu.SemaphoreType.DMA((len(pieces),)),
            pltpu.SemaphoreType.DMA((3,)),
        ],
        compiler_params=pltpu.CompilerParams(vmem_limit_bytes=24 * 2**20),
        cost_estimate=pl.CostEstimate(
            flops=6 * total * width * hidden,
            bytes_accessed=4 * total * width + 6 * hidden * width,
            transcendentals=total * hidden,
        ),
    )(*blocks, *in_hbm(gate_t, up_t, down), *before)


def plus(one, *more):
    total = one.astype(f32)
    for other in more:
        total = total + other.astype(f32)
    return total.astype(bf16)


PIECES = ((0, 1, 7), (2, 6), (3, 4, 5))


def gather_a(rows):
    ring = {0: rows}
    up = down = rows
    for k in range(1, 5):
        up = shift(up, "z", 1)
        ring[NZ - k] = up
        if k < 4:
            down = shift(down, "z", -1)
            ring[k] = down
    own, left, right = [], [], []
    for piece in PIECES:
        own.append(stack([ring[j] for j in piece], *left[-1:], *right[-1:]))
        left.append(shift(own[-1], "x", 1))
        right.append(shift(own[-1], "x", -1))
    far = [shift(left[0], "x", 1), shift(left[1], "x", 1), shift(right[2], "x", -1)]
    return own, left, right, far


def scatter_a(own, left, right, far, other, mark):
    left, right = list(left), list(right)
    back = shift(far[2], "x", -1)
    back, left[0], left[1], _ = lax.optimization_barrier((back, left[0], left[1], mark))
    left[2] = plus(left[2], back)
    right[1] = plus(right[1], shift(far[1], "x", 1))
    right[0] = plus(right[0], shift(far[0], "x", 1))
    at = {}
    for q in (2, 1, 0):
        total = plus(own[q], shift(right[q], "x", 1), shift(left[q], "x", -1))
        if q == 0:
            total, other = lax.optimization_barrier((total, other))
        group = total.shape[0] // len(PIECES[q])
        for i, j in enumerate(PIECES[q]):
            at[j] = total[i * group : (i + 1) * group]
    up, down = shift(at[4], "z", 1), shift(at[5], "z", -1)
    for j in (3, 2, 1):
        up = shift(plus(at[j], up), "z", 1)
        if j > 1:
            down = shift(plus(at[9 - j], down), "z", -1)
    return plus(at[0], up, down), other


def gather_b(rows, *before):
    own = stack([rows] + [shift(rows, "x", by) for by in (-1, 2, 1)], *before)
    return lax.all_gather(own, "z", axis=0, tiled=True)


def scatter_x(total):
    group = total.shape[0] // NX
    own, right, far, left = [total[i * group : (i + 1) * group] for i in range(NX)]
    return plus(own, shift(right, "x", 1), shift(left, "x", -1), shift(far, "x", 2))


def local(
    queries,
    key_vecs,
    values,
    seq_lengths,
    head_gain,
    out_weight,
    residual,
    norm_gain,
    expert_ids,
    gate_weights,
    gate_weight,
    up_weight,
    down_weight,
):
    tok_rows, seq_count, head_width = queries.shape
    head_count = head_width // HDIM
    model_width = residual.shape[-1]
    query_heads = queries.reshape(tok_rows, seq_count, head_count, HDIM)
    key_heads = key_vecs.reshape(tok_rows, seq_count, head_count, HDIM)
    value_heads = values.reshape(tok_rows, seq_count, head_count, HDIM)
    position = lax.axis_index(CTX) * tok_rows + jnp.arange(tok_rows, dtype=jnp.int32)
    live_keys = position[:, None] < seq_lengths[None, :]
    key_heads = jnp.where(live_keys[:, :, None, None], key_heads, jnp.zeros_like(key_heads))
    head_gains = head_gain.astype(f32).reshape(head_count, HDIM)
    state = jnp.einsum("jshd,jshe->shde", key_heads, value_heads, preferred_element_type=f32)
    prior_state = prior_sums(state)
    normed = attend(query_heads, key_heads, value_heads, prior_state, head_gains)
    attended = normed.reshape(tok_rows, seq_count, head_width)
    projected = jnp.einsum(
        "rsk,kd->rsd", attended, out_weight, preferred_element_type=f32
    ).astype(bf16)
    pieces = lax.all_to_all(projected, EXP, split_axis=0, concat_axis=0, tiled=True)
    attn_proj = jnp.sum(pieces.reshape((EXPERTS,) + residual.shape).astype(f32), axis=0)
    stream = residual.astype(f32) + attn_proj
    inv_norm = lax.rsqrt(jnp.mean(stream * stream, axis=-1, keepdims=True) + epsilon)
    moe_in = (stream * inv_norm * norm_gain.astype(f32)).astype(bf16)
    tokens = moe_in.reshape(-1, model_width)
    tok_count = tokens.shape[0]
    total_rows = EXPERTS * MOST
    route_ids = expert_ids.reshape(tok_count * 2)
    order = jnp.arange(tok_count * 2)
    same = (route_ids[:, None] == route_ids[None, :]) & (order[:, None] > order[None, :])
    slots = (route_ids * MOST + jnp.sum(same.astype(jnp.int32), axis=1)).reshape(tok_count, 2)
    target = jnp.arange(total_rows, dtype=jnp.int32)
    hits = slots[:, :, None] == target[None, None, :]
    picker = jnp.sum(hits.astype(f32), axis=1).astype(bf16)
    blend = jnp.sum(
        gate_weights.reshape(tok_count, 2)[:, :, None] * hits.astype(f32), axis=1
    )
    outgoing = lax.dot_general(
        picker, tokens, (((0,), (0,)), ((), ())), preferred_element_type=f32
    ).astype(bf16)
    arrived = lax.all_to_all(outgoing, EXP, split_axis=0, concat_axis=0, tiled=True)

    weights = (gate_weight[0].T, up_weight[0].T, down_weight[0])
    cut = total_rows * 2 // 3
    own, left, right, far = gather_a(arrived[:cut])
    b_rows = gather_b(arrived[cut:], own[0])
    early = expert(own + left[:2] + right[:2], *weights, 288, right[2])
    late = expert(far + left[2:] + right[2:], *weights, 224, *in_hbm(early[0]))
    (b_sums,) = expert(in_hbm(b_rows), *weights, 256, *in_hbm(late[0]))
    mark = b_sums[:8, :HDIM]
    b_sums = lax.psum_scatter(b_sums, "z", scatter_dimension=0, tiled=True)
    a_sums, b_sums = scatter_a(
        early[:3], early[3:5] + late[3:4], early[5:7] + late[4:5], late[:3], b_sums, mark
    )
    summed = jnp.concatenate([a_sums, scatter_x(b_sums)], axis=0)
    returned = lax.all_to_all(summed, EXP, split_axis=0, concat_axis=0, tiled=True)
    moe_out = jnp.dot(blend, returned.astype(f32), precision=lax.Precision.HIGHEST)
    return (stream + moe_out.reshape(stream.shape)).astype(bf16)


def solution(mesh):
    split = Mesh(mesh.devices.reshape(NX, NZ, NY, NC), CTX + EXP)
    each = P(CTX + EXP, None, None)
    return jax.shard_map(
        local,
        mesh=split,
        in_specs=(
            P(CTX, None, EXP),
            P(CTX, None, EXP),
            P(CTX, None, EXP),
            P(),
            P(EXP),
            P(EXP, None),
            each,
            P(),
            each,
            each,
            P(EXP, None, CTX),
            P(EXP, None, CTX),
            P(EXP, CTX, None),
        ),
        out_specs=each,
        check_vma=False,
    )
```

```python
import math

import jax
import jax.numpy as jnp
from jax import lax
from jax.experimental import pallas as pl
from jax.experimental.pallas import tpu as pltpu
from jax.sharding import Mesh, PartitionSpec as P

HDIM = 128
NX, NZ, NY, NC = 4, 8, 4, 2
CTX, EXP = ("x", "z"), ("y", "c")
EXPERTS = NY * NC
MOST = 6

epsilon = 1e-05
bf16, f32 = jnp.bfloat16, jnp.float32


def shift(block, axis, by):
    count = {"x": NX, "z": NZ}[axis]
    return lax.ppermute(block, axis, [(i, (i + by) % count) for i in range(count)])


def prior_sums(state):
    blocks = NX * NZ
    parts = state.astype(bf16).reshape(blocks, -1, HDIM)
    mine = lax.all_to_all(parts, CTX, split_axis=0, concat_axis=0, tiled=True)
    earlier = (jnp.arange(blocks)[:, None] > jnp.arange(blocks)[None, :]).astype(bf16)
    sums = lax.dot_general(
        earlier, mine, (((1,), (0,)), ((), ())), preferred_element_type=f32
    ).astype(bf16)
    back = lax.all_to_all(sums, CTX, split_axis=0, concat_axis=0, tiled=True)
    return back.reshape(state.shape)


def attend(queries, keys, values, prior, gains):
    scores = jnp.einsum("ishd,jshd->shij", queries, keys, preferred_element_type=f32)
    length = queries.shape[0]
    causal = jnp.arange(length)[:, None] >= jnp.arange(length)[None, :]
    weights = jnp.where(causal, scores, 0.0).astype(bf16)
    within = jnp.einsum("shij,jshd->ishd", weights, values, preferred_element_type=f32)
    across = jnp.einsum("ishd,shde->ishe", queries, prior, preferred_element_type=f32)
    mixed = within + across
    scale = lax.rsqrt(jnp.mean(mixed * mixed, axis=-1, keepdims=True) + epsilon)
    return (mixed * scale * gains).astype(bf16)


HBM = pl.BlockSpec(memory_space=pltpu.HBM)


def in_hbm(*arrays):
    return [pltpu.with_memory_space_constraint(x, pltpu.HBM) for x in arrays]


def stack(parts, *before):
    rows, width = parts[0].shape

    def body(*refs):
        out, sems = refs[-2:]
        copies = [
            pltpu.make_async_copy(refs[i], out.at[i], sems.at[i]) for i in range(len(parts))
        ]
        for copy in copies:
            copy.start()
        for copy in copies:
            copy.wait()

    whole = pl.pallas_call(
        body,
        out_shape=jax.ShapeDtypeStruct((len(parts), rows, width), parts[0].dtype),
        in_specs=[HBM] * (len(parts) + len(before)),
        out_specs=pl.BlockSpec(memory_space=pltpu.VMEM),
        scratch_shapes=[pltpu.SemaphoreType.DMA((len(parts),))],
        compiler_params=pltpu.CompilerParams(vmem_limit_bytes=8 * 2**20),
        cost_estimate=pl.CostEstimate(
            flops=0, bytes_accessed=4 * len(parts) * rows * width, transcendentals=0
        ),
    )(*parts, *before)
    return whole.reshape(-1, width)


NT = (((1,), (1,)), ((), ()))


def expert(blocks, gate_t, up_t, down, at_once, *before):
    width, hidden = gate_t.shape[1], gate_t.shape[0]
    tall = [b.shape[0] for b in blocks]
    total = sum(tall)
    chunk = math.gcd(at_once, *tall)
    pieces = [(i, r) for i, rows in enumerate(tall) for r in range(0, rows, chunk)]
    steps = total // at_once
    wide = 512

    def body(*refs):
        n = len(blocks)
        ins, weights, outs = refs[:n], refs[n : n + 3], refs[-n - 8 : -8]
        x, y, wg, wu, wd, in_sem, out_sem, w_sem = refs[-8:]
        loads = [
            pltpu.make_async_copy(
                ins[i].at[pl.ds(r, chunk)], x.at[pl.ds(k * chunk, chunk)], in_sem.at[k]
            )
            for k, (i, r) in enumerate(pieces)
        ]
        stores = [
            pltpu.make_async_copy(
                y.at[pl.ds(k * chunk, chunk)], outs[i].at[pl.ds(r, chunk)], out_sem.at[k]
            )
            for k, (i, r) in enumerate(pieces)
        ]
        fetch = [
            pltpu.make_async_copy(src, dst, w_sem.at[k])
            for k, (src, dst) in enumerate(zip(weights, (wg, wu, wd)))
        ]
        each = at_once // chunk
        fetch[0].start()
        for load in loads[:each]:
            load.start()
        fetch[1].start()
        fetch[2].start()
        for load in loads[each:]:
            load.start()
        for s in range(steps):
            for load in loads[s * each : (s + 1) * each]:
                load.wait()
            rows = pl.ds(s * at_once, at_once)
            if s == 0:
                fetch[0].wait()
            gate = lax.dot_general(x[rows, :], wg[...], NT, preferred_element_type=f32)
            if s == 0:
                fetch[1].wait()
            up = lax.dot_general(x[rows, :], wu[...], NT, preferred_element_type=f32)
            acts = (gate / (1.0 + jnp.exp(-gate)) * up).astype(bf16)
            if s == 0:
                fetch[2].wait()
            for c in range(0, width, wide):
                y[rows, pl.ds(c, wide)] = jnp.dot(
                    acts, wd[:, pl.ds(c, wide)], preferred_element_type=f32
                ).astype(bf16)
            for store in stores[s * each : (s + 1) * each]:
                store.start()
        for store in stores:
            store.wait()

    return pl.pallas_call(
        body,
        out_shape=[pltpu.HBM(b.shape, bf16) for b in blocks],
        in_specs=[HBM] * (len(blocks) + 3 + len(before)),
        out_specs=[HBM] * len(blocks),
        scratch_shapes=[
            pltpu.VMEM((total, width), bf16),
            pltpu.VMEM((total, width), bf16),
            pltpu.VMEM((hidden, width), bf16),
            pltpu.VMEM((hidden, width), bf16),
            pltpu.VMEM((hidden, width), bf16),
            pltpu.SemaphoreType.DMA((len(pieces),)),
            pltpu.SemaphoreType.DMA((len(pieces),)),
            pltpu.SemaphoreType.DMA((3,)),
        ],
        compiler_params=pltpu.CompilerParams(vmem_limit_bytes=24 * 2**20),
        cost_estimate=pl.CostEstimate(
            flops=6 * total * width * hidden,
            bytes_accessed=4 * total * width + 6 * hidden * width,
            transcendentals=total * hidden,
        ),
    )(*blocks, *in_hbm(gate_t, up_t, down), *before)


def plus(one, *more):
    total = one.astype(f32)
    for other in more:
        total = total + other.astype(f32)
    return total.astype(bf16)


PIECES = ((0, 1, 7), (2, 6), (3, 4, 5))


def gather_a(rows):
    ring = {0: rows}
    up = down = rows
    for k in range(1, 5):
        up = shift(up, "z", 1)
        ring[NZ - k] = up
        if k < 4:
            down = shift(down, "z", -1)
            ring[k] = down
    own, left, right = [], [], []
    for piece in PIECES:
        own.append(stack([ring[j] for j in piece], *left[-1:], *right[-1:]))
        left.append(shift(own[-1], "x", 1))
        right.append(shift(own[-1], "x", -1))
    far = [shift(left[0], "x", 1), shift(left[1], "x", 1), shift(right[2], "x", -1)]
    return own, left, right, far


def scatter_a(own, left, right, far, other):
    left, right = list(left), list(right)
    back = shift(far[2], "x", -1)
    back, left[0], left[1] = lax.optimization_barrier((back, left[0], left[1]))
    left[2] = plus(left[2], back)
    right[1] = plus(right[1], shift(far[1], "x", 1))
    right[0] = plus(right[0], shift(far[0], "x", 1))
    at = {}
    for q in (2, 1, 0):
        total = plus(own[q], shift(right[q], "x", 1), shift(left[q], "x", -1))
        group = total.shape[0] // len(PIECES[q])
        for i, j in enumerate(PIECES[q]):
            at[j] = total[i * group : (i + 1) * group]
    up, down = shift(at[4], "z", 1), shift(at[5], "z", -1)
    for j in (3, 2, 1):
        up = shift(plus(at[j], up), "z", 1)
        if j > 1:
            down = shift(plus(at[9 - j], down), "z", -1)
    return plus(at[0], up, down), other


def gather_b(rows, *before):
    own = stack([rows] + [shift(rows, "x", by) for by in (-1, 2, 1)], *before)
    return lax.all_gather(own, "z", axis=0, tiled=True)


def scatter_x(total):
    group = total.shape[0] // NX
    own, right, far, left = [total[i * group : (i + 1) * group] for i in range(NX)]
    return plus(own, shift(right, "x", 1), shift(left, "x", -1), shift(far, "x", 2))


def local(
    queries,
    key_vecs,
    values,
    seq_lengths,
    head_gain,
    out_weight,
    residual,
    norm_gain,
    expert_ids,
    gate_weights,
    gate_weight,
    up_weight,
    down_weight,
):
    tok_rows, seq_count, head_width = queries.shape
    head_count = head_width // HDIM
    model_width = residual.shape[-1]
    query_heads = queries.reshape(tok_rows, seq_count, head_count, HDIM)
    key_heads = key_vecs.reshape(tok_rows, seq_count, head_count, HDIM)
    value_heads = values.reshape(tok_rows, seq_count, head_count, HDIM)
    position = lax.axis_index(CTX) * tok_rows + jnp.arange(tok_rows, dtype=jnp.int32)
    live_keys = position[:, None] < seq_lengths[None, :]
    key_heads = jnp.where(live_keys[:, :, None, None], key_heads, jnp.zeros_like(key_heads))
    head_gains = head_gain.astype(f32).reshape(head_count, HDIM)
    state = jnp.einsum("jshd,jshe->shde", key_heads, value_heads, preferred_element_type=f32)
    prior_state = prior_sums(state)
    normed = attend(query_heads, key_heads, value_heads, prior_state, head_gains)
    attended = normed.reshape(tok_rows, seq_count, head_width)
    projected = jnp.einsum(
        "rsk,kd->rsd", attended, out_weight, preferred_element_type=f32
    ).astype(bf16)
    pieces = lax.all_to_all(projected, EXP, split_axis=0, concat_axis=0, tiled=True)
    attn_proj = jnp.sum(pieces.reshape((EXPERTS,) + residual.shape).astype(f32), axis=0)
    stream = residual.astype(f32) + attn_proj
    inv_norm = lax.rsqrt(jnp.mean(stream * stream, axis=-1, keepdims=True) + epsilon)
    moe_in = (stream * inv_norm * norm_gain.astype(f32)).astype(bf16)
    tokens = moe_in.reshape(-1, model_width)
    tok_count = tokens.shape[0]
    total_rows = EXPERTS * MOST
    route_ids = expert_ids.reshape(tok_count * 2)
    order = jnp.arange(tok_count * 2)
    same = (route_ids[:, None] == route_ids[None, :]) & (order[:, None] > order[None, :])
    slots = (route_ids * MOST + jnp.sum(same.astype(jnp.int32), axis=1)).reshape(tok_count, 2)
    target = jnp.arange(total_rows, dtype=jnp.int32)
    hits = slots[:, :, None] == target[None, None, :]
    picker = jnp.sum(hits.astype(f32), axis=1).astype(bf16)
    blend = jnp.sum(
        gate_weights.reshape(tok_count, 2)[:, :, None] * hits.astype(f32), axis=1
    )
    outgoing = lax.dot_general(
        picker, tokens, (((0,), (0,)), ((), ())), preferred_element_type=f32
    ).astype(bf16)
    arrived = lax.all_to_all(outgoing, EXP, split_axis=0, concat_axis=0, tiled=True)

    weights = (gate_weight[0].T, up_weight[0].T, down_weight[0])
    cut = total_rows * 2 // 3
    own, left, right, far = gather_a(arrived[:cut])
    b_rows = gather_b(arrived[cut:], own[0])
    early = expert(own + left[:2] + right[:2], *weights, 288)
    (b_sums,) = expert(in_hbm(b_rows), *weights, 256, *in_hbm(early[0]), right[2])
    late = expert(far + left[2:] + right[2:], *weights, 224, *in_hbm(b_sums))
    b_sums = lax.psum_scatter(b_sums, "z", scatter_dimension=0, tiled=True)
    a_sums, b_sums = scatter_a(
        early[:3], early[3:5] + late[3:4], early[5:7] + late[4:5], late[:3], b_sums
    )
    summed = jnp.concatenate([a_sums, scatter_x(b_sums)], axis=0)
    returned = lax.all_to_all(summed, EXP, split_axis=0, concat_axis=0, tiled=True)
    moe_out = jnp.dot(blend, returned.astype(f32), precision=lax.Precision.HIGHEST)
    return (stream + moe_out.reshape(stream.shape)).astype(bf16)


def solution(mesh):
    split = Mesh(mesh.devices.reshape(NX, NZ, NY, NC), CTX + EXP)
    each = P(CTX + EXP, None, None)
    return jax.shard_map(
        local,
        mesh=split,
        in_specs=(
            P(CTX, None, EXP),
            P(CTX, None, EXP),
            P(CTX, None, EXP),
            P(),
            P(EXP),
            P(EXP, None),
            each,
            P(),
            each,
            each,
            P(EXP, None, CTX),
            P(EXP, None, CTX),
            P(EXP, CTX, None),
        ),
        out_specs=each,
        check_vma=False,
    )
```

```python
import math

import jax
import jax.numpy as jnp
from jax import lax
from jax.experimental import pallas as pl
from jax.experimental.pallas import tpu as pltpu
from jax.sharding import Mesh, PartitionSpec as P

HDIM = 128
NX, NZ, NY, NC = 4, 8, 4, 2
CTX, EXP = ("x", "z"), ("y", "c")
EXPERTS = NY * NC
MOST = 6

epsilon = 1e-05
bf16, f32 = jnp.bfloat16, jnp.float32


def shift(block, axis, by):
    count = {"x": NX, "z": NZ}[axis]
    return lax.ppermute(block, axis, [(i, (i + by) % count) for i in range(count)])


def prior_sums(state):
    blocks = NX * NZ
    parts = state.astype(bf16).reshape(blocks, -1, HDIM)
    mine = lax.all_to_all(parts, CTX, split_axis=0, concat_axis=0, tiled=True)
    earlier = (jnp.arange(blocks)[:, None] > jnp.arange(blocks)[None, :]).astype(bf16)
    sums = lax.dot_general(
        earlier, mine, (((1,), (0,)), ((), ())), preferred_element_type=f32
    ).astype(bf16)
    back = lax.all_to_all(sums, CTX, split_axis=0, concat_axis=0, tiled=True)
    return back.reshape(state.shape)


def attend(queries, keys, values, prior, gains):
    scores = jnp.einsum("ishd,jshd->shij", queries, keys, preferred_element_type=f32)
    length = queries.shape[0]
    causal = jnp.arange(length)[:, None] >= jnp.arange(length)[None, :]
    weights = jnp.where(causal, scores, 0.0).astype(bf16)
    within = jnp.einsum("shij,jshd->ishd", weights, values, preferred_element_type=f32)
    across = jnp.einsum("ishd,shde->ishe", queries, prior, preferred_element_type=f32)
    mixed = within + across
    scale = lax.rsqrt(jnp.mean(mixed * mixed, axis=-1, keepdims=True) + epsilon)
    return (mixed * scale * gains).astype(bf16)


HBM = pl.BlockSpec(memory_space=pltpu.HBM)


def in_hbm(*arrays):
    return [pltpu.with_memory_space_constraint(x, pltpu.HBM) for x in arrays]


def stack(parts, *before):
    rows, width = parts[0].shape

    def body(*refs):
        out, sems = refs[-2:]
        copies = [
            pltpu.make_async_copy(refs[i], out.at[i], sems.at[i]) for i in range(len(parts))
        ]
        for copy in copies:
            copy.start()
        for copy in copies:
            copy.wait()

    whole = pl.pallas_call(
        body,
        out_shape=jax.ShapeDtypeStruct((len(parts), rows, width), parts[0].dtype),
        in_specs=[HBM] * (len(parts) + len(before)),
        out_specs=pl.BlockSpec(memory_space=pltpu.VMEM),
        scratch_shapes=[pltpu.SemaphoreType.DMA((len(parts),))],
        compiler_params=pltpu.CompilerParams(vmem_limit_bytes=8 * 2**20),
        cost_estimate=pl.CostEstimate(
            flops=0, bytes_accessed=4 * len(parts) * rows * width, transcendentals=0
        ),
    )(*parts, *before)
    return whole.reshape(-1, width)


NT = (((1,), (1,)), ((), ()))


def expert(blocks, gate_t, up_t, down, at_once, *before):
    width, hidden = gate_t.shape[1], gate_t.shape[0]
    tall = [b.shape[0] for b in blocks]
    total = sum(tall)
    chunk = math.gcd(at_once, *tall)
    pieces = [(i, r) for i, rows in enumerate(tall) for r in range(0, rows, chunk)]
    steps = total // at_once
    wide = 512

    def body(*refs):
        n = len(blocks)
        ins, weights, outs = refs[:n], refs[n : n + 3], refs[-n - 8 : -8]
        x, y, wg, wu, wd, in_sem, out_sem, w_sem = refs[-8:]
        loads = [
            pltpu.make_async_copy(
                ins[i].at[pl.ds(r, chunk)], x.at[pl.ds(k * chunk, chunk)], in_sem.at[k]
            )
            for k, (i, r) in enumerate(pieces)
        ]
        stores = [
            pltpu.make_async_copy(
                y.at[pl.ds(k * chunk, chunk)], outs[i].at[pl.ds(r, chunk)], out_sem.at[k]
            )
            for k, (i, r) in enumerate(pieces)
        ]
        fetch = [
            pltpu.make_async_copy(src, dst, w_sem.at[k])
            for k, (src, dst) in enumerate(zip(weights, (wg, wu, wd)))
        ]
        each = at_once // chunk
        fetch[0].start()
        for load in loads[:each]:
            load.start()
        fetch[1].start()
        fetch[2].start()
        for load in loads[each:]:
            load.start()
        for s in range(steps):
            for load in loads[s * each : (s + 1) * each]:
                load.wait()
            rows = pl.ds(s * at_once, at_once)
            if s == 0:
                fetch[0].wait()
            gate = lax.dot_general(x[rows, :], wg[...], NT, preferred_element_type=f32)
            if s == 0:
                fetch[1].wait()
            up = lax.dot_general(x[rows, :], wu[...], NT, preferred_element_type=f32)
            acts = (gate / (1.0 + jnp.exp(-gate)) * up).astype(bf16)
            if s == 0:
                fetch[2].wait()
            for c in range(0, width, wide):
                y[rows, pl.ds(c, wide)] = jnp.dot(
                    acts, wd[:, pl.ds(c, wide)], preferred_element_type=f32
                ).astype(bf16)
            for store in stores[s * each : (s + 1) * each]:
                store.start()
        for store in stores:
            store.wait()

    return pl.pallas_call(
        body,
        out_shape=[pltpu.HBM(b.shape, bf16) for b in blocks],
        in_specs=[HBM] * (len(blocks) + 3 + len(before)),
        out_specs=[HBM] * len(blocks),
        scratch_shapes=[
            pltpu.VMEM((total, width), bf16),
            pltpu.VMEM((total, width), bf16),
            pltpu.VMEM((hidden, width), bf16),
            pltpu.VMEM((hidden, width), bf16),
            pltpu.VMEM((hidden, width), bf16),
            pltpu.SemaphoreType.DMA((len(pieces),)),
            pltpu.SemaphoreType.DMA((len(pieces),)),
            pltpu.SemaphoreType.DMA((3,)),
        ],
        compiler_params=pltpu.CompilerParams(vmem_limit_bytes=24 * 2**20),
        cost_estimate=pl.CostEstimate(
            flops=6 * total * width * hidden,
            bytes_accessed=4 * total * width + 6 * hidden * width,
            transcendentals=total * hidden,
        ),
    )(*blocks, *in_hbm(gate_t, up_t, down), *before)


def plus(one, *more):
    total = one.astype(f32)
    for other in more:
        total = total + other.astype(f32)
    return total.astype(bf16)


PIECES = ((0, 1, 7), (2, 6), (3, 4, 5))


def gather_a(rows):
    ring = {0: rows}
    up = down = rows
    for k in range(1, 5):
        up = shift(up, "z", 1)
        ring[NZ - k] = up
        if k < 4:
            down = shift(down, "z", -1)
            ring[k] = down
    own, left, right = [], [], []
    for piece in PIECES:
        own.append(stack([ring[j] for j in piece], *left[-1:], *right[-1:]))
        left.append(shift(own[-1], "x", 1))
        right.append(shift(own[-1], "x", -1))
    far = [shift(left[0], "x", 1), shift(left[1], "x", 1), shift(right[2], "x", -1)]
    return own, left, right, far


def scatter_a(own, left, right, far, other):
    left, right = list(left), list(right)
    back = shift(far[2], "x", -1)
    back, left[0], left[1] = lax.optimization_barrier((back, left[0], left[1]))
    left[2] = plus(left[2], back)
    right[1] = plus(right[1], shift(far[1], "x", 1))
    right[0] = plus(right[0], shift(far[0], "x", 1))
    at = {}
    for q in (2, 1, 0):
        total = plus(own[q], shift(right[q], "x", 1), shift(left[q], "x", -1))
        if q == 2:
            total, other = lax.optimization_barrier((total, other))
        group = total.shape[0] // len(PIECES[q])
        for i, j in enumerate(PIECES[q]):
            at[j] = total[i * group : (i + 1) * group]
    up, down = shift(at[4], "z", 1), shift(at[5], "z", -1)
    for j in (3, 2, 1):
        up = shift(plus(at[j], up), "z", 1)
        if j > 1:
            down = shift(plus(at[9 - j], down), "z", -1)
    return plus(at[0], up, down), other


def gather_b(rows, *before):
    own = stack([rows] + [shift(rows, "x", by) for by in (-1, 2, 1)], *before)
    return lax.all_gather(own, "z", axis=0, tiled=True)


def scatter_x(total):
    group = total.shape[0] // NX
    own, right, far, left = [total[i * group : (i + 1) * group] for i in range(NX)]
    return plus(own, shift(right, "x", 1), shift(left, "x", -1), shift(far, "x", 2))


def local(
    queries,
    key_vecs,
    values,
    seq_lengths,
    head_gain,
    out_weight,
    residual,
    norm_gain,
    expert_ids,
    gate_weights,
    gate_weight,
    up_weight,
    down_weight,
):
    tok_rows, seq_count, head_width = queries.shape
    head_count = head_width // HDIM
    model_width = residual.shape[-1]
    query_heads = queries.reshape(tok_rows, seq_count, head_count, HDIM)
    key_heads = key_vecs.reshape(tok_rows, seq_count, head_count, HDIM)
    value_heads = values.reshape(tok_rows, seq_count, head_count, HDIM)
    position = lax.axis_index(CTX) * tok_rows + jnp.arange(tok_rows, dtype=jnp.int32)
    live_keys = position[:, None] < seq_lengths[None, :]
    key_heads = jnp.where(live_keys[:, :, None, None], key_heads, jnp.zeros_like(key_heads))
    head_gains = head_gain.astype(f32).reshape(head_count, HDIM)
    state = jnp.einsum("jshd,jshe->shde", key_heads, value_heads, preferred_element_type=f32)
    prior_state = prior_sums(state)
    normed = attend(query_heads, key_heads, value_heads, prior_state, head_gains)
    attended = normed.reshape(tok_rows, seq_count, head_width)
    projected = jnp.einsum(
        "rsk,kd->rsd", attended, out_weight, preferred_element_type=f32
    ).astype(bf16)
    pieces = lax.all_to_all(projected, EXP, split_axis=0, concat_axis=0, tiled=True)
    attn_proj = jnp.sum(pieces.reshape((EXPERTS,) + residual.shape).astype(f32), axis=0)
    stream = residual.astype(f32) + attn_proj
    inv_norm = lax.rsqrt(jnp.mean(stream * stream, axis=-1, keepdims=True) + epsilon)
    moe_in = (stream * inv_norm * norm_gain.astype(f32)).astype(bf16)
    tokens = moe_in.reshape(-1, model_width)
    tok_count = tokens.shape[0]
    total_rows = EXPERTS * MOST
    route_ids = expert_ids.reshape(tok_count * 2)
    order = jnp.arange(tok_count * 2)
    same = (route_ids[:, None] == route_ids[None, :]) & (order[:, None] > order[None, :])
    slots = (route_ids * MOST + jnp.sum(same.astype(jnp.int32), axis=1)).reshape(tok_count, 2)
    target = jnp.arange(total_rows, dtype=jnp.int32)
    hits = slots[:, :, None] == target[None, None, :]
    picker = jnp.sum(hits.astype(f32), axis=1).astype(bf16)
    blend = jnp.sum(
        gate_weights.reshape(tok_count, 2)[:, :, None] * hits.astype(f32), axis=1
    )
    outgoing = lax.dot_general(
        picker, tokens, (((0,), (0,)), ((), ())), preferred_element_type=f32
    ).astype(bf16)
    arrived = lax.all_to_all(outgoing, EXP, split_axis=0, concat_axis=0, tiled=True)

    weights = (gate_weight[0].T, up_weight[0].T, down_weight[0])
    cut = total_rows * 2 // 3
    own, left, right, far = gather_a(arrived[:cut])
    b_rows = gather_b(arrived[cut:], own[0])
    early = expert(own + left[:2] + right[:2], *weights, 288, right[2])
    (b_sums,) = expert(in_hbm(b_rows), *weights, 256, *in_hbm(early[0]), *far, left[2])
    late = expert(far + left[2:] + right[2:], *weights, 448, *in_hbm(b_sums))
    b_sums = lax.psum_scatter(b_sums, "z", scatter_dimension=0, tiled=True)
    a_sums, b_sums = scatter_a(
        early[:3], early[3:5] + late[3:4], early[5:7] + late[4:5], late[:3], b_sums
    )
    summed = jnp.concatenate([a_sums, scatter_x(b_sums)], axis=0)
    returned = lax.all_to_all(summed, EXP, split_axis=0, concat_axis=0, tiled=True)
    moe_out = jnp.dot(blend, returned.astype(f32), precision=lax.Precision.HIGHEST)
    return (stream + moe_out.reshape(stream.shape)).astype(bf16)


def solution(mesh):
    split = Mesh(mesh.devices.reshape(NX, NZ, NY, NC), CTX + EXP)
    each = P(CTX + EXP, None, None)
    return jax.shard_map(
        local,
        mesh=split,
        in_specs=(
            P(CTX, None, EXP),
            P(CTX, None, EXP),
            P(CTX, None, EXP),
            P(),
            P(EXP),
            P(EXP, None),
            each,
            P(),
            each,
            each,
            P(EXP, None, CTX),
            P(EXP, None, CTX),
            P(EXP, CTX, None),
        ),
        out_specs=each,
        check_vma=False,
    )
```
